32 devices in a mesh: dp: 2 (over x), expert: 4 (over y, core), tensor: 4 (over z).
Axes of the slice: x: 2, y: 2, z: 4, core: 2. Of those that a mesh axis runs over, the one named last changes fastest.
Arguments:
- hidden_in: bfloat16 [1024, 1024], P(('dp', 'expert')), may hold values from -6 to 6
- seq_lengths: int32 [8, 3], P(('dp', 'expert')), may hold values from 1 to 96, 128 in all within a row
- expert_routes: int32 [1024, 8], P(('dp', 'expert')), may hold values from 0 to 31, all different within a row; in each aligned block of 128 rows (0 to 127, 128 to 255, ...) at most 48 rows name the same one
- first_gain: bfloat16 [1024], replicated, may hold values from 0.5 to 1.5
- query_weight: bfloat16 [1024, 1024], P(None, 'tensor'), may hold values from -0.1875 to 0.1875
- key_weight: bfloat16 [1024, 512], P(None, 'tensor'), may hold values from -0.1875 to 0.1875
- value_weight: bfloat16 [1024, 512], P(None, 'tensor'), may hold values from -0.1875 to 0.1875
- output_weight: bfloat16 [1024, 1024], P(None, 'tensor'), may hold values from -0.5 to 0.5
- second_gain: bfloat16 [1024], replicated, may hold values from 0.5 to 1.5
- router_weight: bfloat16 [1024, 32], replicated, may hold values from -0.09375 to 0.09375
- gate_weight: bfloat16 [32, 1024, 512], P('expert', None, 'tensor'), may hold values from -0.1875 to 0.1875
- up_weight: bfloat16 [32, 1024, 512], P('expert', None, 'tensor'), may hold values from -0.1875 to 0.1875
- down_weight: bfloat16 [32, 1024, 512], P('expert', None, 'tensor'), may hold values from -1 to 1
- grad_layer_out: bfloat16 [1024, 1024], P(('dp', 'expert')), may hold values from -6 to 6
Outputs:
- layer_out: bfloat16 [1024, 1024], P(('dp', 'expert'))
- grad_input: float32 [1024, 1024], P(('dp', 'expert'))
- grad_first_gain: float32 [1024], P(('dp', 'expert'))
- grad_query: float32 [1024, 1024], P(('dp', 'expert'), 'tensor')
- grad_key: float32 [1024, 512], P(('dp', 'expert'), 'tensor')
- grad_value: float32 [1024, 512], P(('dp', 'expert'), 'tensor')
- grad_outproj: float32 [1024, 1024], P(('dp', 'expert'), 'tensor')
- grad_second_gain: float32 [1024], P(('dp', 'expert'))
- grad_router: float32 [1024, 32], P(('dp', 'expert'))
- grad_gate: float32 [32, 1024, 512], P('expert', 'dp', 'tensor')
- grad_upproj: float32 [32, 1024, 512], P('expert', 'dp', 'tensor')
- grad_down: float32 [32, 1024, 512], P('expert', 'dp', 'tensor')
The draws below stay inside these ranges and needn't reach their ends.
Inputs may be any that keep to these rules, and one draw needn't show every extreme that they name: `expert_routes`: among the 128 rows of one token group, each expert is named at most 48 times.
All inputs are finite; a program needn't handle non-finite values.
Results may differ from the reference program's by a relative error of at most 0.017.
Values may be sent and summed in bfloat16 or wider, within the bound.
No kernel may reach another device: no remote copies, remote signals or barrier semaphores. Data moves between devices by JAX's collectives and lax.ppermute only.
A program may use at most 128 MiB of HBM per device.

```python
import math
import jax
import jax.numpy as jnp
import numpy as np
from jax import lax

D = 1024
HQ = 16
HK = 8
HD = 64
FFE = 512
EXPERTS = 32
TOP = 8
TOK_DEV = 128
NSEQ = 3
GROUPS = 8
TOKENS = 1024
CAP = 48
MAXLEN = 96


def levels(stream_key, shape, split, least, high):
    factor_of = 1.0
    for axis_at, shards_of in split:
        draws = jax.random.uniform(jax.random.fold_in(jax.random.fold_in(stream_key, 6), axis_at), (shards_of,), jnp.float32, least / len(split), high / len(split))
        factor_of = factor_of * jnp.repeat(jnp.exp(draws), shape[axis_at] // shards_of).reshape((-1,) + (1,) * (len(shape) - 1 - axis_at))
    return factor_of


def profile(number_of, total, limit, slope):
    weights = [(1 << 20) // math.isqrt(grade ** slope) + 1 for grade in range(2, number_of + 1)]
    surplus, holding = total - limit - (number_of - 1), [1] * (number_of - 1)
    while surplus > 0:
        candidates = [i for i in range(number_of - 1) if holding[i] < limit]
        pool, left = sum([weights[i] for i in candidates]), surplus
        for i in candidates:
            extra = min(limit - holding[i], max(1, left * weights[i] // pool), surplus)
            holding[i] = holding[i] + extra
            surplus = surplus - extra
    return np.array([limit] + holding)


def ragged(own_key, amount, total, most, lean):
    if amount == 2:
        one = jax.random.randint(own_key, (), max(1, total - most), min(most, total - 1) + 1)
        return jnp.stack([one, total - one])
    lengths = jnp.asarray(profile(amount, total, most, lean), jnp.int32)
    pairs = (amount - 1) // 2
    source_of, receiver = lengths[1:1 + 2 * pairs:2], lengths[2:2 + 2 * pairs:2]
    room = jnp.minimum(source_of - 1, most - receiver)
    moved = jax.random.randint(jax.random.fold_in(own_key, 1), (pairs,), 0, 1 << 20) % (room + 1)
    lengths = lengths.at[1:1 + 2 * pairs:2].set(source_of - moved).at[2:2 + 2 * pairs:2].set(receiver + moved)
    return lengths[jax.random.permutation(jax.random.fold_in(own_key, 2), amount)]


def deal_out(stream_key, own, number, rows, amount, top, limit, slope):
    ranking = jax.random.permutation(stream_key, amount)
    heavy_load, ordinary = shares(amount, rows * top, limit, slope, True), shares(amount, rows * top, limit, slope, False)
    places = jnp.arange(amount)

    def named(sizes, offset_by):
        used = int((sizes > 0).sum())
        fixed = max(1, used // 4)
        shifted = fixed + (places - fixed + offset_by * (used - fixed)) % max(1, amount - fixed)
        return jnp.zeros((amount,), jnp.int32).at[ranking[jnp.where(places < fixed, places, shifted)]].set(jnp.asarray(sizes, jnp.int32))

    sizes = jnp.where(number % 4 == 0, named(heavy_load, number // 4), named(ordinary, number - number // 4 - 1))
    mixed = jax.random.permutation(jax.random.fold_in(own, 3), amount)
    donor, sink = mixed[0:amount // 2 * 2:2], mixed[1:amount // 2 * 2:2]
    room = jnp.minimum(sizes[donor] - 1, limit - sizes[sink]) // 2
    room = jnp.where((donor == ranking[0]) | (sink == ranking[0]) | (sizes[sink] == 0), 0, jnp.maximum(room, 0))
    shifted = jax.random.randint(jax.random.fold_in(own, 4), (amount // 2,), 0, 1 << 20) % (room + 1)
    sizes = sizes.at[donor].add(-shifted).at[sink].add(shifted)
    items = jnp.searchsorted(jnp.cumsum(sizes), jnp.arange(rows * top), side="right").astype(jnp.int32)
    listing = items.reshape(top, rows).T
    listing = listing[jax.random.permutation(jax.random.fold_in(own, 1), rows)]
    offset_by = jax.random.randint(jax.random.fold_in(own, 2), (rows, 1), 0, top)
    return jnp.take_along_axis(listing, (jnp.arange(top)[None, :] + offset_by) % top, axis=1)


def shares(count, total, reach, lean, full):
    portions = [(1 << 20) // math.isqrt(rank ** lean) + 1 for rank in range(1, count + 1)]
    largest = reach if full else min(reach, max(-(-total // count), total * portions[0] // sum(portions)))
    least = 1 if total - largest >= count - 1 else 0
    counts, rest = [largest] + [least] * (count - 1), total - largest - least * (count - 1)
    while rest > 0:
        candidates = [i for i in range(1, count) if counts[i] < largest] or [i for i in range(1, count) if counts[i] < reach]
        pool, left = sum([portions[i] for i in candidates]), rest
        for i in candidates:
            addition = min(reach - counts[i], max(1, left * portions[i] // pool), rest)
            counts[i] = counts[i] + addition
            rest = rest - addition
    return np.array(counts)


def gaussian(rng, extent, scale, reach, cuts=(), kind=jnp.bfloat16):
    factor_of = levels(rng, extent, cuts, -0.22, 0.18) if cuts else 1.0
    values = jax.random.normal(rng, extent, jnp.float32) * scale * factor_of
    return jnp.minimum(jnp.maximum(values, -reach), reach).astype(kind)


def setup_inputs(seed: int = 0) -> dict:
    seeds = jax.random.split(jax.random.key(seed), 15)
    hidden_in = gaussian(seeds[0], (TOKENS, D), 1.0, 6.0, ((0, 8),))
    seq_lengths = jax.vmap(lambda own: ragged(own, NSEQ, TOK_DEV, MAXLEN, 1))(jax.random.split(seeds[1], GROUPS)).reshape((GROUPS, NSEQ)).astype(jnp.int32)
    expert_routes_keys = jax.random.split(jax.random.fold_in(seeds[2], 1), TOKENS // TOK_DEV)
    expert_routes_turns = jax.random.permutation(jax.random.fold_in(seeds[2], 3), TOKENS // TOK_DEV)
    expert_routes = jax.vmap(lambda own, number: deal_out(jax.random.fold_in(seeds[2], 2), own, number, TOK_DEV, EXPERTS, TOP, CAP, 1))(expert_routes_keys, expert_routes_turns).reshape((TOKENS, TOP))
    first_gain = jnp.clip(1.0 + 0.1 * jax.random.normal(seeds[3], (D,), jnp.float32), 0.5, 1.5).astype(jnp.bfloat16)
    query_weight = gaussian(seeds[4], (D, HQ * HD), D ** -0.5, 0.1875, ((1, 4),))
    key_weight = gaussian(seeds[5], (D, HK * HD), D ** -0.5, 0.1875, ((1, 4),))
    value_weight = gaussian(seeds[6], (D, HK * HD), D ** -0.5, 0.1875, ((1, 4),))
    output_weight = gaussian(seeds[7], (D, HQ * HD), (HQ * HD // 8) ** -0.5, 0.5, ((1, 4),))
    second_gain = jnp.clip(1.0 + 0.1 * jax.random.normal(seeds[8], (D,), jnp.float32), 0.5, 1.5).astype(jnp.bfloat16)
    router_weight = gaussian(seeds[9], (D, EXPERTS), (4 * D) ** -0.5, 0.09375)
    gate_weight = gaussian(seeds[10], (EXPERTS, D, FFE), D ** -0.5, 0.1875, ((0, 4), (2, 4)))
    up_weight = gaussian(seeds[11], (EXPERTS, D, FFE), D ** -0.5, 0.1875, ((0, 4), (2, 4)))
    down_weight = gaussian(seeds[12], (EXPERTS, D, FFE), (FFE // 16) ** -0.5, 1.0, ((0, 4), (2, 4)))
    grad_layer_out = gaussian(seeds[13], (TOKENS, D), 1.0, 6.0, ((0, 8),))
    return {"hidden_in": hidden_in, "seq_lengths": seq_lengths, "expert_routes": expert_routes, "first_gain": first_gain, "query_weight": query_weight, "key_weight": key_weight, "value_weight": value_weight, "output_weight": output_weight, "second_gain": second_gain, "router_weight": router_weight, "gate_weight": gate_weight, "up_weight": up_weight, "down_weight": down_weight, "grad_layer_out": grad_layer_out}


EPSILON = 1e-06

@jax.custom_vjp
def low(v):
    return lax.optimization_barrier(v.astype(jnp.bfloat16)).astype(jnp.float32)

@jax.custom_vjp
def low_back(v):
    return v

def low_keep(v):
    return (low(v), None)

def low_pass(kept, grad):
    return (grad,)

def back_keep(v):
    return (v, None)

def back_low(kept, grad):
    return (low(grad),)
low.defvjp(low_keep, low_pass)
low_back.defvjp(back_keep, back_low)

def matmul(left, right):
    return jnp.dot(left, right, precision=lax.Precision.HIGHEST, preferred_element_type=jnp.float32)

def rope_tables(positions, head_size):
    inverse = jnp.exp(jnp.arange(head_size // 2).astype(jnp.float32) * (-2.0 * math.log(10000.0) / head_size))
    angles = positions.astype(jnp.float32)[:, None] * inverse[None, :]
    return (jnp.cos(angles)[:, None, :], jnp.sin(angles)[:, None, :])

def rotate(values, cosine_table, sine_table):
    half_size = values.shape[-1] // 2
    lower_half = values[..., :half_size]
    upper_half = values[..., half_size:]
    return jnp.concatenate([lower_half * cosine_table - upper_half * sine_table, upper_half * cosine_table + lower_half * sine_table], -1)

def norm_rows(values, gain_vector):
    scale_rows = lax.rsqrt(lax.optimization_barrier(jnp.mean(values * values, -1, keepdims=True)) + EPSILON)
    return values * scale_rows * gain_vector

def token_places(seq_lengths):
    row_ids = jnp.arange(TOKENS, dtype=jnp.int32)
    group_index = row_ids // TOK_DEV
    local_row = row_ids % TOK_DEV
    ends_at = jnp.cumsum(seq_lengths, 1, dtype=jnp.int32)[group_index]
    segment = lax.optimization_barrier(jnp.sum((local_row[:, None] >= ends_at).astype(jnp.int32), 1, dtype=jnp.int32))
    starts_at = ends_at - seq_lengths[group_index]
    chosen = segment[:, None] == jnp.arange(NSEQ, dtype=jnp.int32)[None, :]
    start_row = lax.optimization_barrier(jnp.sum(jnp.where(chosen, starts_at, 0), 1, dtype=jnp.int32))
    return (segment, local_row - start_row)

def attend_group(blocks):
    queries, keys_rot, values_low, segment = blocks
    expanded_keys = jnp.repeat(keys_rot, HQ // HK, axis=1)
    expanded_values = jnp.repeat(values_low, HQ // HK, axis=1)
    scores = low_back(jnp.einsum('thd,uhd->htu', queries, expanded_keys, precision=lax.Precision.HIGHEST) * HD ** (-0.5))
    positions_in = jnp.arange(TOK_DEV, dtype=jnp.int32)
    allowed = (segment[:, None] == segment[None, :]) & (positions_in[None, :] <= positions_in[:, None])
    masked = jnp.where(allowed[None], scores, -1e+30)
    top_score = lax.optimization_barrier(jnp.max(masked, -1, keepdims=True))
    exponent = jnp.exp(masked - top_score)
    probabilities = low(exponent / lax.optimization_barrier(jnp.sum(exponent, -1, keepdims=True)))
    return jnp.einsum('htu,uhd->thd', probabilities, expanded_values, precision=lax.Precision.HIGHEST)

def expert_rows(second_normed, gates_flat):

    def run_expert(blocks):
        route_ids, live_rows, gate_w, up_w, down_w = blocks
        inputs = second_normed[route_ids // TOP]
        gate_proj = low_back(matmul(inputs, gate_w))
        up_proj = low_back(matmul(inputs, up_w))
        hidden_units = low(jax.nn.silu(gate_proj) * up_proj)
        outputs = low_back(matmul(hidden_units, down_w.T))
        weights_now = jnp.where(live_rows, gates_flat[route_ids], 0.0)
        return outputs * weights_now[:, None]
    return run_expert

def reference(hidden_in, seq_lengths, expert_routes, first_gain, query_weight, key_weight, value_weight, output_weight, second_gain, router_weight, gate_weight, up_weight, down_weight, grad_layer_out):
    segment, positions = token_places(seq_lengths)
    cosine_table, sine_table = rope_tables(positions, HD)
    flat_experts = expert_routes.reshape(-1)
    rows_most = TOKENS // TOK_DEV * CAP
    expert_ids = jnp.arange(EXPERTS, dtype=jnp.int32)

    def routes_of(expert_id):
        return jnp.nonzero(flat_experts == expert_id, size=rows_most, fill_value=0)[0].astype(jnp.int32)
    route_table = lax.map(routes_of, expert_ids)
    expert_load = lax.optimization_barrier(jnp.sum((flat_experts[None, :] == expert_ids[:, None]).astype(jnp.int32), 1, dtype=jnp.int32))
    live_table = jnp.arange(rows_most, dtype=jnp.int32)[None, :] < expert_load[:, None]
    token_table = route_table // TOP
    picked = expert_routes[:, :, None] == expert_ids[None, None, :]
    groups = TOKENS // TOK_DEV

    def forward(hidden_float, gain_one, query_w, key_w, value_w, output_w, gain_two, router_w, gate_w, up_w, down_w):
        first_normed = low(norm_rows(hidden_float, gain_one))
        query_pre = low_back(matmul(first_normed, query_w)).reshape(TOKENS, HQ, HD)
        key_pre = low_back(matmul(first_normed, key_w)).reshape(TOKENS, HK, HD)
        queries = low(rotate(query_pre, cosine_table, sine_table))
        keys_rot = low(rotate(key_pre, cosine_table, sine_table))
        values_low = low_back(low(matmul(first_normed, value_w))).reshape(TOKENS, HK, HD)
        attended = lax.map(jax.checkpoint(attend_group), (queries.reshape(groups, TOK_DEV, HQ, HD), keys_rot.reshape(groups, TOK_DEV, HK, HD), values_low.reshape(groups, TOK_DEV, HK, HD), segment.reshape(groups, TOK_DEV)))
        attended = low_back(low(attended.reshape(TOKENS, HQ * HD)))
        residual = hidden_float + low_back(matmul(attended, output_w.T))
        second_normed = low(norm_rows(residual, gain_two))
        logits = matmul(second_normed, router_w)
        route_logits = lax.optimization_barrier(jnp.sum(jnp.where(picked, logits[:, None, :], 0.0), -1))
        route_gates = jax.nn.softmax(route_logits, -1)
        outputs = lax.map(jax.checkpoint(expert_rows(second_normed, route_gates.reshape(-1))), (route_table, live_table, gate_w, up_w, down_w))
        expert_mix = jnp.zeros_like(residual).at[token_table.reshape(-1)].add(outputs.reshape(-1, D))
        return residual + expert_mix
    floats = (hidden_in.astype(jnp.float32), first_gain.astype(jnp.float32), query_weight.astype(jnp.float32), key_weight.astype(jnp.float32), value_weight.astype(jnp.float32), output_weight.astype(jnp.float32), second_gain.astype(jnp.float32), router_weight.astype(jnp.float32), gate_weight.astype(jnp.float32), up_weight.astype(jnp.float32), down_weight.astype(jnp.float32))
    layer_out, pullback = jax.vjp(forward, *floats)
    gradients = pullback(grad_layer_out.astype(jnp.float32))
    return (layer_out.astype(jnp.bfloat16), gradients[0], gradients[1], gradients[2], gradients[3], gradients[4], gradients[5], gradients[6], gradients[7], gradients[8], gradients[9], gradients[10])
```

```python
import math

import jax
import jax.numpy as jnp
from jax import lax
from jax.sharding import PartitionSpec as P

HD = 64
EPSILON = 1e-06
F32 = jnp.float32
BF16 = jnp.bfloat16
HIGH = lax.Precision.HIGHEST


def rope_tables(positions, head_size):
    inverse = jnp.exp(
        jnp.arange(head_size // 2).astype(F32) * (-2.0 * math.log(10000.0) / head_size)
    )
    angles = positions.astype(F32)[:, None] * inverse[None, :]
    return (jnp.cos(angles)[:, None, :], jnp.sin(angles)[:, None, :])


def rotate(values, cosine_table, sine_table):
    half_size = values.shape[-1] // 2
    lower_half = values[..., :half_size]
    upper_half = values[..., half_size:]
    return jnp.concatenate(
        [
            lower_half * cosine_table - upper_half * sine_table,
            upper_half * cosine_table + lower_half * sine_table,
        ],
        -1,
    )


def positions_of(lengths_row, row_ids):
    ends_at = [lengths_row[0]]
    for i in range(1, lengths_row.shape[0]):
        ends_at.append(ends_at[-1] + lengths_row[i])
    ends_at = jnp.stack(ends_at)
    segment = jnp.sum((row_ids[:, None] >= ends_at[None, :]).astype(jnp.int32), 1, dtype=jnp.int32)
    starts_at = ends_at - lengths_row
    chosen = segment[:, None] == jnp.arange(lengths_row.shape[0], dtype=jnp.int32)[None, :]
    start_row = jnp.sum(jnp.where(chosen, starts_at[None, :], 0), 1, dtype=jnp.int32)
    return (segment, row_ids - start_row)


def dot(left, right, dims, **kw):
    return lax.dot_general(left, right, (dims, ((), ())), preferred_element_type=F32, **kw)


def swap(x, axis, k):
    n = lax.axis_size(axis)
    return lax.ppermute(x, axis, [(i, i ^ k) for i in range(n)])


def bits_of(n):
    k, out = n // 2, []
    while k >= 1:
        out.append(k)
        k //= 2
    return out


def gather_expert(x, axis=0):
    for k in bits_of(lax.axis_size("expert")):
        x = jnp.concatenate([x, swap(x, "expert", k)], axis)
    return x


def reduce_expert(x, dtype, axis=0):
    for k in reversed(bits_of(lax.axis_size("expert"))):
        half = x.shape[axis] // 2
        keep = lax.slice_in_dim(x, 0, half, axis=axis)
        sent = lax.slice_in_dim(x, half, 2 * half, axis=axis).astype(dtype)
        x = keep.astype(F32) + swap(sent, "expert", k).astype(F32)
        x = x.astype(dtype)
    return x


def reduce_tensor(x, dtype, axis=0):
    n = lax.axis_size("tensor")
    rows = x.shape[axis] // n
    blocks = [lax.slice_in_dim(x, k * rows, (k + 1) * rows, axis=axis) for k in range(n)]
    total = blocks[0].astype(F32)
    for k in range(1, n):
        total = total + swap(blocks[k].astype(dtype), "tensor", k).astype(F32)
    return total


def gather_tensor(x):
    n = lax.axis_size("tensor")
    return [x] + [swap(x, "tensor", k) for k in range(1, n)]


def by_distance(x, me, n):
    blocks = x.reshape((n, x.shape[0] // n) + x.shape[1:])
    return jnp.concatenate(
        [lax.dynamic_index_in_dim(blocks, me ^ k, 0, keepdims=False) for k in range(n)], 0
    )


def reduce_plane(x):
    places = lax.axis_size("dp"), lax.axis_size("expert")
    width = x.shape[1]
    rows = x.shape[0] // (places[0] * places[1])
    expert_bits = bits_of(places[1])
    me = lax.axis_index("expert")
    x = x.reshape((places[0],) + (2,) * len(expert_bits) + (rows, width))
    for k in reversed(expert_bits):
        at = x.ndim - 3
        bit = (me // k) % 2
        keep = lax.dynamic_index_in_dim(x, bit, at, keepdims=False)
        sent = lax.dynamic_index_in_dim(x, 1 - bit, at, keepdims=False)
        shape = keep.shape
        got = swap(sent.astype(BF16).reshape(-1, width), "expert", k).reshape(shape)
        x = keep + got.astype(F32)
    mine = lax.axis_index("dp")
    total = lax.dynamic_index_in_dim(x, mine, 0, keepdims=False)
    for k in range(1, places[0]):
        sent = lax.dynamic_index_in_dim(x, mine ^ k, 0, keepdims=False)
        total = total + swap(sent.astype(BF16), "dp", k).astype(F32)
    return total


def on_device(
    hidden_in,
    seq_lengths,
    expert_routes,
    first_gain,
    query_weight,
    key_weight,
    value_weight,
    output_weight,
    second_gain,
    router_weight,
    gate_weight,
    up_weight,
    down_weight,
    grad_layer_out,
):
    tokens_here, model_width = hidden_in.shape
    query_heads = query_weight.shape[1] // HD
    kv_heads = key_weight.shape[1] // HD
    group_size = query_heads // kv_heads
    expert_count = router_weight.shape[1]
    local_experts, _, units = gate_weight.shape
    tensor_n = lax.axis_size("tensor")
    expert_n = lax.axis_size("expert")
    dp_n = lax.axis_size("dp")
    me_t, me_e, me_d = (lax.axis_index(a) for a in ("tensor", "expert", "dp"))
    block = tokens_here // tensor_n
    score_scale = HD ** (-0.5)

    hidden_rel = by_distance(hidden_in, me_t, tensor_n)
    grad_rel = by_distance(grad_layer_out, me_t, tensor_n)
    routes_rel = by_distance(expert_routes, me_t, tensor_n)
    row_ids = (
        ((jnp.arange(tensor_n, dtype=jnp.int32) ^ me_t) * block)[:, None]
        + jnp.arange(block, dtype=jnp.int32)[None, :]
    ).reshape(-1)

    expert_ids = jnp.arange(expert_count, dtype=jnp.int32)
    routed = jnp.sum((routes_rel[:, :, None] == expert_ids).astype(F32), 1).astype(BF16)
    grad_far = [swap(grad_rel, "dp", k) for k in range(1, dp_n)]
    routed_far = [swap(routed, "dp", k) for k in range(1, dp_n)]
    grad_sets = [gather_expert(g) for g in [grad_rel] + grad_far]
    routed_sets = [gather_expert(g) for g in [routed] + routed_far]

    hidden_float = hidden_rel.astype(F32)
    first_scale = lax.rsqrt(jnp.mean(hidden_float * hidden_float, -1, keepdims=True) + EPSILON)
    first_hat = hidden_float * first_scale
    first_float = first_gain.astype(F32)
    first_normed = (first_hat * first_float).astype(BF16)
    segment, positions = positions_of(seq_lengths[0], row_ids)
    cosine_table, sine_table = rope_tables(positions, HD)
    query_pre = dot(first_normed, query_weight, ((1,), (0,))).reshape(tokens_here, query_heads, HD)
    key_pre = dot(first_normed, key_weight, ((1,), (0,))).reshape(tokens_here, kv_heads, HD)
    queries = rotate(query_pre, cosine_table, sine_table).astype(BF16)
    keys_rot = rotate(key_pre, cosine_table, sine_table).astype(BF16)
    values_low = (
        dot(first_normed, value_weight, ((1,), (0,)))
        .astype(BF16)
        .reshape(tokens_here, kv_heads, HD)
    )
    grouped = queries.reshape(tokens_here, kv_heads, group_size, HD)
    scores = (
        jnp.einsum("tkgd,ukd->kgtu", grouped, keys_rot, preferred_element_type=F32) * score_scale
    )
    allowed = (segment[:, None] == segment[None, :]) & (row_ids[None, :] <= row_ids[:, None])
    masked = jnp.where(allowed, scores, -1e30)
    top_score = jnp.max(masked, -1, keepdims=True)
    exponent = jnp.exp(masked - top_score)
    probabilities = exponent / jnp.sum(exponent, -1, keepdims=True)
    probs_low = probabilities.astype(BF16)
    attended = (
        jnp.einsum("kgtu,ukd->tkgd", probs_low, values_low, preferred_element_type=F32)
        .astype(BF16)
        .reshape(tokens_here, query_heads * HD)
    )
    attn_part = dot(attended, output_weight, ((1,), (1,)))
    attn_out = reduce_tensor(attn_part, BF16)

    residual = hidden_float[:block] + attn_out
    second_scale = lax.rsqrt(jnp.mean(residual * residual, -1, keepdims=True) + EPSILON)
    second_hat = residual * second_scale
    second_float = second_gain.astype(F32)
    second_block = (second_hat * second_float).astype(BF16)
    second_group = jnp.concatenate(gather_tensor(second_block), 0)
    second_sets = [gather_expert(second_group)] + [
        gather_expert(swap(second_group, "dp", k)) for k in range(1, dp_n)
    ]

    def gates_of(normed, routed_here):
        logits = dot(normed, router_weight, ((1,), (0,)))
        logits = jnp.where(routed_here > 0, logits, -1e30)
        weights = jnp.exp(logits - jnp.max(logits, -1, keepdims=True))
        return weights / jnp.sum(weights, -1, keepdims=True)

    def expert_side(normed, routed_here, grad_here):
        gates = gates_of(normed, routed_here)
        mine = lax.dynamic_slice_in_dim(gates, me_e * local_experts, local_experts, 1)
        raw = jnp.einsum("td,edf->tef", grad_here, down_weight, preferred_element_type=F32)
        gate_proj = jnp.einsum("td,edf->tef", normed, gate_weight, preferred_element_type=F32)
        up_proj = jnp.einsum("td,edf->tef", normed, up_weight, preferred_element_type=F32)
        sigmoid_gate = jax.nn.sigmoid(gate_proj)
        activated = gate_proj * sigmoid_gate
        hidden = activated * up_proj
        grad_hidden = raw * mine[:, :, None]
        grad_gate_proj = (
            grad_hidden * up_proj * sigmoid_gate * (1.0 + gate_proj * (1.0 - sigmoid_gate))
        ).astype(BF16)
        grad_up_proj = (grad_hidden * activated).astype(BF16)
        gated = (hidden * mine[:, :, None]).astype(BF16)
        return gates, mine, raw, hidden, gated, grad_gate_proj, grad_up_proj

    sides = [
        expert_side(second_sets[i], routed_sets[i], grad_sets[i]) for i in range(dp_n)
    ]
    gates, mine, raw, hidden, gated, grad_gate_proj, grad_up_proj = sides[0]
    grad_arrival = jnp.einsum(
        "tef,edf->td", grad_gate_proj, gate_weight, preferred_element_type=F32
    ) + jnp.einsum("tef,edf->td", grad_up_proj, up_weight, preferred_element_type=F32)
    grad_arrival = grad_arrival.astype(BF16)
    grad_gates_mine = jnp.sum(raw * hidden, -1).T
    grad_gates = lax.dynamic_update_slice_in_dim(
        jnp.zeros((expert_count, grad_gates_mine.shape[1]), F32),
        grad_gates_mine,
        me_e * local_experts,
        0,
    )
    grad_routed = reduce_tensor(reduce_expert(grad_arrival, BF16), BF16)
    grad_gates = reduce_tensor(reduce_expert(grad_gates, F32, 1), F32, 1).T
    if tokens_here * expert_n > 1024:
        gated, grad_routed = lax.optimization_barrier((gated, grad_routed))
    mixed = jnp.einsum("tef,edf->td", gated, down_weight, preferred_element_type=F32)
    mixed = mixed.astype(BF16)
    mixed = reduce_tensor(reduce_expert(mixed, BF16), BF16)
    layer_block = (residual + mixed).astype(BF16)

    half = model_width // dp_n

    def weight_grad(lefts, rights):
        return sum(
            jnp.einsum(
                "td,tef->edf",
                lax.dynamic_slice_in_dim(left, me_d * half, half, 1),
                right,
                preferred_element_type=F32,
            )
            for left, right in zip(lefts, rights)
        )

    grad_gate = weight_grad(second_sets, [s[5] for s in sides])
    grad_upproj = weight_grad(second_sets, [s[6] for s in sides])
    grad_down = weight_grad(grad_sets, [s[4] for s in sides])

    gates_block = gates[:block]
    grad_logits = gates_block * (
        grad_gates - jnp.sum(gates_block * grad_gates, -1, keepdims=True)
    )
    grad_second = grad_routed + dot(
        grad_logits, router_weight.astype(F32), ((1,), (1,)), precision=HIGH
    )
    second_gained = grad_second * second_float
    grad_resid = grad_rel[:block].astype(F32) + second_scale * (
        second_gained - second_hat * jnp.mean(second_gained * second_hat, -1, keepdims=True)
    )
    grad_out_low = jnp.concatenate(gather_tensor(grad_resid.astype(BF16)), 0)
    grad_logits_all = jnp.concatenate(gather_tensor(grad_logits), 0)
    grad_second_gain = sum(gather_tensor(jnp.sum(grad_second * second_hat, 0)))
    grad_router = dot(second_group.astype(F32), grad_logits_all, ((0,), (0,)), precision=HIGH)

    grad_outproj = reduce_plane(dot(grad_out_low, attended, ((0,), (0,))))
    grad_attended = (
        dot(grad_out_low, output_weight, ((1,), (0,)))
        .astype(BF16)
        .reshape(tokens_here, kv_heads, group_size, HD)
    )
    grad_probs = jnp.einsum(
        "tkgd,ukd->kgtu", grad_attended, values_low, preferred_element_type=F32
    )
    grad_values = (
        jnp.einsum("kgtu,tkgd->ukd", probs_low, grad_attended, preferred_element_type=F32)
        .astype(BF16)
        .reshape(tokens_here, kv_heads * HD)
    )
    grad_scores = (
        probabilities * (grad_probs - jnp.sum(probabilities * grad_probs, -1, keepdims=True))
    ).astype(BF16)
    grad_queries = (
        jnp.einsum("kgtu,ukd->tkgd", grad_scores, keys_rot, preferred_element_type=F32)
        * score_scale
    )
    grad_keys = (
        jnp.einsum("kgtu,tkgd->ukd", grad_scores, grouped, preferred_element_type=F32)
        * score_scale
    )
    grad_query_pre = (
        rotate(grad_queries.reshape(tokens_here, query_heads, HD), cosine_table, -sine_table)
        .astype(BF16)
        .reshape(tokens_here, query_heads * HD)
    )
    grad_key_pre = (
        rotate(grad_keys, cosine_table, -sine_table)
        .astype(BF16)
        .reshape(tokens_here, kv_heads * HD)
    )
    grad_first = (
        dot(grad_query_pre, query_weight, ((1,), (1,)))
        + dot(grad_key_pre, key_weight, ((1,), (1,)))
        + dot(grad_values, value_weight, ((1,), (1,)))
    )
    grad_first_part = jnp.sum(grad_first * first_hat, 0)
    grad_first = reduce_tensor(grad_first, BF16)
    first_gained = grad_first * first_float
    hat_block = first_hat[:block]
    grad_input = grad_resid + first_scale[:block] * (
        first_gained - hat_block * jnp.mean(first_gained * hat_block, -1, keepdims=True)
    )
    last = jnp.concatenate(
        [
            dot(first_normed, grad_query_pre, ((0,), (0,))),
            dot(first_normed, grad_key_pre, ((0,), (0,))),
            dot(first_normed, grad_values, ((0,), (0,))),
            grad_router,
            grad_second_gain[:, None],
            grad_first_part[:, None],
        ],
        1,
    )
    last = reduce_plane(last)
    marks = [0]
    for w in (query_heads * HD, kv_heads * HD, kv_heads * HD, expert_count, 1, 1):
        marks.append(marks[-1] + w)
    grad_query, grad_key, grad_value, grad_router, grad_second_out, grad_first_out = (
        last[:, marks[i] : marks[i + 1]] for i in range(6)
    )
    grad_first_out = sum(gather_tensor(grad_first_out[:, 0]))

    layer_out = by_distance(jnp.concatenate(gather_tensor(layer_block), 0), me_t, tensor_n)
    grad_input = by_distance(
        jnp.concatenate(gather_tensor(grad_input.astype(BF16)), 0), me_t, tensor_n
    ).astype(F32)
    return (
        layer_out,
        grad_input,
        grad_first_out,
        grad_query,
        grad_key,
        grad_value,
        grad_outproj,
        grad_second_out[:, 0],
        grad_router,
        grad_gate,
        grad_upproj,
        grad_down,
    )


def solution(mesh):
    tokens = P(("dp", "expert"), None)
    columns = P(None, "tensor")
    experts = P("expert", None, "tensor")
    rows = P(("dp", "expert"))
    both = P(("dp", "expert"), "tensor")
    expert_grads = P("expert", "dp", "tensor")
    return jax.shard_map(
        on_device,
        mesh=mesh,
        in_specs=(tokens, tokens, tokens, P())
        + (columns,) * 4
        + (P(), P())
        + (experts,) * 3
        + (tokens,),
        out_specs=(tokens, tokens, rows)
        + (both,) * 4
        + (rows, tokens)
        + (expert_grads,) * 3,
        check_vma=False,
    )
```

```python
import functools
import math

import jax
import jax.numpy as jnp
from jax import lax
from jax.experimental import pallas as pl
from jax.experimental.pallas import tpu as pltpu
from jax.sharding import PartitionSpec as P

HD = 64
EPSILON = 1e-06
F32 = jnp.float32
BF16 = jnp.bfloat16
HIGH = lax.Precision.HIGHEST


def rope_tables(positions, head_size):
    inverse = jnp.exp(
        jnp.arange(head_size // 2).astype(F32) * (-2.0 * math.log(10000.0) / head_size)
    )
    angles = positions.astype(F32)[:, None] * inverse[None, :]
    return (jnp.cos(angles)[:, None, :], jnp.sin(angles)[:, None, :])


def rotate(values, cosine_table, sine_table):
    half_size = values.shape[-1] // 2
    lower_half = values[..., :half_size]
    upper_half = values[..., half_size:]
    return jnp.concatenate(
        [
            lower_half * cosine_table - upper_half * sine_table,
            upper_half * cosine_table + lower_half * sine_table,
        ],
        -1,
    )


def positions_of(lengths_row, row_ids):
    ends_at = [lengths_row[0]]
    for i in range(1, lengths_row.shape[0]):
        ends_at.append(ends_at[-1] + lengths_row[i])
    ends_at = jnp.stack(ends_at)
    segment = jnp.sum((row_ids[:, None] >= ends_at[None, :]).astype(jnp.int32), 1, dtype=jnp.int32)
    starts_at = ends_at - lengths_row
    chosen = segment[:, None] == jnp.arange(lengths_row.shape[0], dtype=jnp.int32)[None, :]
    start_row = jnp.sum(jnp.where(chosen, starts_at[None, :], 0), 1, dtype=jnp.int32)
    return (segment, row_ids - start_row)


def dot(left, right, dims, **kw):
    return lax.dot_general(left, right, (dims, ((), ())), preferred_element_type=F32, **kw)


def swap(x, axis, k):
    n = lax.axis_size(axis)
    return lax.ppermute(x, axis, [(i, i ^ k) for i in range(n)])


def bits_of(n):
    k, out = n // 2, []
    while k >= 1:
        out.append(k)
        k //= 2
    return out


def gather_expert(x, axis=0):
    for k in bits_of(lax.axis_size("expert")):
        x = jnp.concatenate([x, swap(x, "expert", k)], axis)
    return x


def reduce_expert(x, dtype, axis=0):
    for k in reversed(bits_of(lax.axis_size("expert"))):
        half = x.shape[axis] // 2
        keep = lax.slice_in_dim(x, 0, half, axis=axis)
        sent = lax.slice_in_dim(x, half, 2 * half, axis=axis).astype(dtype)
        x = keep.astype(F32) + swap(sent, "expert", k).astype(F32)
        x = x.astype(dtype)
    return x


def reduce_tensor(x, dtype, axis=0):
    n = lax.axis_size("tensor")
    rows = x.shape[axis] // n
    blocks = [lax.slice_in_dim(x, k * rows, (k + 1) * rows, axis=axis) for k in range(n)]
    total = blocks[0].astype(F32)
    for k in range(1, n):
        total = total + swap(blocks[k].astype(dtype), "tensor", k).astype(F32)
    return total


def gather_tensor(x):
    n = lax.axis_size("tensor")
    return [x] + [swap(x, "tensor", k) for k in range(1, n)]


def by_distance(x, me, n):
    blocks = x.reshape((n, x.shape[0] // n) + x.shape[1:])
    return jnp.concatenate(
        [lax.dynamic_index_in_dim(blocks, me ^ k, 0, keepdims=False) for k in range(n)], 0
    )


def reduce_plane(x):
    places = lax.axis_size("dp"), lax.axis_size("expert")
    width = x.shape[1]
    rows = x.shape[0] // (places[0] * places[1])
    expert_bits = bits_of(places[1])
    me = lax.axis_index("expert")
    x = x.reshape((places[0],) + (2,) * len(expert_bits) + (rows, width))
    for k in reversed(expert_bits):
        at = x.ndim - 3
        bit = (me // k) % 2
        keep = lax.dynamic_index_in_dim(x, bit, at, keepdims=False)
        sent = lax.dynamic_index_in_dim(x, 1 - bit, at, keepdims=False)
        shape = keep.shape
        got = swap(sent.astype(BF16).reshape(-1, width), "expert", k).reshape(shape)
        x = keep + got.astype(F32)
    mine = lax.axis_index("dp")
    total = lax.dynamic_index_in_dim(x, mine, 0, keepdims=False)
    for k in range(1, places[0]):
        sent = lax.dynamic_index_in_dim(x, mine ^ k, 0, keepdims=False)
        total = total + swap(sent.astype(BF16), "dp", k).astype(F32)
    return total


def pair_of(local_experts):
    return 2 if local_experts % 2 == 0 else 1


def kernel_params(tokens):
    return pltpu.CompilerParams(vmem_limit_bytes=(40 if tokens <= 512 else 60) * 2**20)


def side_by_side(ref, first, count):
    parts = [ref[first + i] for i in range(count)]
    return parts[0] if count == 1 else jnp.concatenate(parts, 1)


def split_rows(chunk, chunks, value, near_ref, far_ref):
    if chunks == 1:
        half = value.shape[0] // 2
        near_ref[...] = value[:half]
        far_ref[...] = value[half:]
        return
    rows = value.shape[0]

    @pl.when(chunk < chunks // 2)
    def _():
        near_ref[pl.ds(pl.multiple_of(chunk * rows, rows), rows), :] = value

    @pl.when(chunk >= chunks // 2)
    def _():
        at = (chunk - chunks // 2) * rows
        far_ref[pl.ds(pl.multiple_of(at, rows), rows), :] = value


def expert_kernel(own, chunks, steps, pair, experts, *refs):
    base_ref, x_ref, dy_ref, gate_ref, up_ref, down_ref, router_ref = refs[:7]
    both_ref, gated_ref = refs[7:9]
    if own:
        near_ref, far_ref = refs[9:11]
        gates_scr, total_scr, dg_scr = refs[11:]
    else:
        (gates_scr,) = refs[9:]
    chunk, step = pl.program_id(0), pl.program_id(1)
    width = x_ref.shape[1]
    lanes = gates_scr.shape[1]

    @pl.when(step == 0)
    def _():
        logits = dot(x_ref[...], router_ref[...], ((1,), (0,)))
        routed = dy_ref[:, width : width + experts].astype(F32) > 0.5
        logits = jnp.where(routed, logits, -1e30)
        weights = jnp.exp(logits - jnp.max(logits, -1, keepdims=True))
        gates_scr[...] = jnp.zeros_like(gates_scr)
        gates_scr[:, :experts] = weights / jnp.sum(weights, -1, keepdims=True)
        if own:
            total_scr[...] = jnp.zeros_like(total_scr)
            dg_scr[...] = jnp.zeros_like(dg_scr)

    first = base_ref[0] + step * pair
    gates = pltpu.roll(gates_scr[...], lax.rem(lanes - first, lanes), 1)
    raw_all = dot(dy_ref[:, :width], side_by_side(down_ref, 0, pair), ((1,), (0,)))
    units = gate_ref.shape[2]
    column = lax.broadcasted_iota(jnp.int32, gates.shape, 1)
    for i in range(pair):
        weight = jnp.concatenate([gate_ref[i], up_ref[i]], 1)
        both = dot(x_ref[...], weight, ((1,), (0,)))
        gate_proj, up_proj = both[:, :units], both[:, units:]
        raw = raw_all[:, i * units : (i + 1) * units]
        mine = gates[:, i : i + 1]
        sigmoid_gate = 0.5 * jnp.tanh(0.5 * gate_proj) + 0.5
        activated = gate_proj * sigmoid_gate
        hidden = activated * up_proj
        grad_hidden = raw * mine
        grad_gate = grad_hidden * up_proj * (sigmoid_gate + activated * (1.0 - sigmoid_gate))
        grads = jnp.concatenate([grad_gate, grad_hidden * activated], 1).astype(BF16)
        both_ref[:, i * 2 * units : (i + 1) * 2 * units] = grads
        gated_ref[:, i * units : (i + 1) * units] = (hidden * mine).astype(BF16)
        if own:
            total_scr[...] += dot(grads, weight, ((1,), (1,)))
            dg = jnp.sum(raw * hidden, 1, keepdims=True)
            dg_scr[...] += jnp.where(column == first + i, dg, 0.0)

    if own:

        @pl.when(step == steps - 1)
        def _():
            dg = dg_scr[...]
            high = dg.astype(BF16).astype(F32)
            low = pltpu.roll(dg - high, experts, 1)
            message = jnp.concatenate([total_scr[...], high + low], 1).astype(BF16)
            split_rows(chunk, chunks, message, near_ref, far_ref)


def expert_call(own, base, x, dy, gate_weight, up_weight, down_weight, router_weight):
    tokens, width = x.shape
    local, _, units = gate_weight.shape
    experts = router_weight.shape[1]
    pair = pair_of(local)
    rows = min(tokens, 512)
    chunks, steps = tokens // rows, local // pair
    grid_spec = dict(
        grid=(chunks, steps),
        in_specs=[
            pl.BlockSpec(memory_space=pltpu.SMEM),
            pl.BlockSpec((rows, width), lambda c, s: (c, 0)),
            pl.BlockSpec((rows, dy.shape[1]), lambda c, s: (c, 0)),
        ]
        + [pl.BlockSpec((pair, width, units), lambda c, s: (s, 0, 0))] * 3
        + [pl.BlockSpec(router_weight.shape, lambda c, s: (0, 0))],
        out_specs=[
            pl.BlockSpec((rows, pair * 2 * units), lambda c, s: (c, s)),
            pl.BlockSpec((rows, pair * units), lambda c, s: (c, s)),
        ],
        scratch_shapes=[pltpu.VMEM((rows, 128), F32)],
    )
    out_shape = [
        jax.ShapeDtypeStruct((tokens, local * 2 * units), BF16),
        jax.ShapeDtypeStruct((tokens, local * units), BF16),
    ]
    if own:
        half = (tokens // 2, width + 128)
        grid_spec["out_specs"] += [pl.BlockSpec(half, lambda c, s: (0, 0))] * 2
        out_shape += [jax.ShapeDtypeStruct(half, BF16)] * 2
        grid_spec["scratch_shapes"] += [
            pltpu.VMEM((rows, width), F32),
            pltpu.VMEM((rows, 128), F32),
        ]
    products = 5 if own else 3
    return pl.pallas_call(
        functools.partial(expert_kernel, own, chunks, steps, pair, experts),
        out_shape=out_shape,
        compiler_params=kernel_params(tokens),
        cost_estimate=pl.CostEstimate(
            flops=2 * products * tokens * width * local * units,
            bytes_accessed=2 * (3 * local * width * units + 3 * tokens * width),
            transcendentals=tokens * local * units,
        ),
        name="experts_own" if own else "experts_far",
        **grid_spec,
    )(base, x, dy, gate_weight, up_weight, down_weight, router_weight)


def mixed_kernel(chunks, steps, pair, gated_ref, down_ref, near_ref, far_ref, total_scr):
    chunk, step = pl.program_id(0), pl.program_id(1)

    @pl.when(step == 0)
    def _():
        total_scr[...] = jnp.zeros_like(total_scr)

    total_scr[...] += dot(gated_ref[...], side_by_side(down_ref, 0, pair), ((1,), (1,)))

    @pl.when(step == steps - 1)
    def _():
        split_rows(chunk, chunks, total_scr[...].astype(BF16), near_ref, far_ref)


def mixed_call(gated, down_weight):
    tokens = gated.shape[0]
    local, width, units = down_weight.shape
    pair = pair_of(local)
    rows = min(tokens, 512)
    chunks, steps = tokens // rows, local // pair
    half = (tokens // 2, width)
    return pl.pallas_call(
        functools.partial(mixed_kernel, chunks, steps, pair),
        grid=(chunks, steps),
        in_specs=[
            pl.BlockSpec((rows, pair * units), lambda c, s: (c, s)),
            pl.BlockSpec((pair, width, units), lambda c, s: (s, 0, 0)),
        ],
        out_specs=[pl.BlockSpec(half, lambda c, s: (0, 0))] * 2,
        out_shape=[jax.ShapeDtypeStruct(half, BF16)] * 2,
        scratch_shapes=[pltpu.VMEM((rows, width), F32)],
        compiler_params=kernel_params(tokens),
        cost_estimate=pl.CostEstimate(
            flops=2 * tokens * width * local * units,
            bytes_accessed=2 * (local * width * units + 2 * tokens * width),
            transcendentals=0,
        ),
        name="experts_mixed",
    )(gated, down_weight)


def weight_grad_kernel(sets, pair, units, place_ref, *refs):
    xs, dys, boths, gateds = (refs[i * sets : (i + 1) * sets] for i in range(4))
    grad_gate_ref, grad_up_ref, grad_down_ref, x_scr, dy_scr = refs[4 * sets :]

    @pl.when(pl.program_id(0) == 0)
    def _():
        for n in range(sets):
            rows = xs[n].shape[0]
            x_scr[:, n * rows : (n + 1) * rows] = xs[n][...].T
            dy_scr[:, n * rows : (n + 1) * rows] = dys[n][...].T

    rows = xs[0].shape[0]
    totals = [None] * pair
    down = None
    for n in range(sets):
        left = x_scr[:, n * rows : (n + 1) * rows]
        for i in range(pair):
            part = dot(left, boths[n][:, i * 2 * units : (i + 1) * 2 * units], ((1,), (0,)))
            totals[i] = part if totals[i] is None else totals[i] + part
        part = dot(dy_scr[:, n * rows : (n + 1) * rows], gateds[n][...], ((1,), (0,)))
        down = part if down is None else down + part
    for i in range(pair):
        grad_gate_ref[i] = totals[i][:, :units]
        grad_up_ref[i] = totals[i][:, units:]
        grad_down_ref[i] = down[:, i * units : (i + 1) * units]


def weight_grad_call(place, xs, dys, boths, gateds, local, units):
    sets = len(xs)
    tokens, width = xs[0].shape
    half = width // sets
    pair = pair_of(local)
    once = pl.Buffered(1)
    grads = jax.ShapeDtypeStruct((local, half, units), F32)
    columns = pl.BlockSpec((tokens, half), lambda s, place: (0, place[0]), pipeline_mode=once)
    return pl.pallas_call(
        functools.partial(weight_grad_kernel, sets, pair, units),
        grid_spec=pltpu.PrefetchScalarGridSpec(
            num_scalar_prefetch=1,
            grid=(local // pair,),
            in_specs=[columns] * (2 * sets)
            + [pl.BlockSpec((tokens, pair * 2 * units), lambda s, place: (0, s))] * sets
            + [pl.BlockSpec((tokens, pair * units), lambda s, place: (0, s))] * sets,
            out_specs=[pl.BlockSpec((pair, half, units), lambda s, place: (s, 0, 0))] * 3,
            scratch_shapes=[pltpu.VMEM((half, sets * tokens), BF16)] * 2,
        ),
        out_shape=[grads] * 3,
        compiler_params=kernel_params(tokens),
        cost_estimate=pl.CostEstimate(
            flops=6 * sets * tokens * half * local * units,
            bytes_accessed=4 * 3 * local * half * units + 8 * sets * tokens * width,
            transcendentals=0,
        ),
        name="experts_weight_grads",
    )(place, *xs, *dys, *boths, *gateds)


def reduce_halves(near, far, dtype):
    bits = list(reversed(bits_of(lax.axis_size("expert"))))
    for k in bits[:-1]:
        got = swap(far, "expert", k)
        half = near.shape[0] // 2
        far = (near[half:].astype(F32) + got[half:].astype(F32)).astype(dtype)
        near = (near[:half].astype(F32) + got[:half].astype(F32)).astype(dtype)
    return near.astype(F32) + swap(far, "expert", bits[-1]).astype(F32)


def on_device(
    hidden_in,
    seq_lengths,
    expert_routes,
    first_gain,
    query_weight,
    key_weight,
    value_weight,
    output_weight,
    second_gain,
    router_weight,
    gate_weight,
    up_weight,
    down_weight,
    grad_layer_out,
):
    tokens_here, model_width = hidden_in.shape
    query_heads = query_weight.shape[1] // HD
    kv_heads = key_weight.shape[1] // HD
    group_size = query_heads // kv_heads
    expert_count = router_weight.shape[1]
    local_experts, _, units = gate_weight.shape
    tensor_n = lax.axis_size("tensor")
    expert_n = lax.axis_size("expert")
    dp_n = lax.axis_size("dp")
    me_t, me_e, me_d = (lax.axis_index(a) for a in ("tensor", "expert", "dp"))
    block = tokens_here // tensor_n
    score_scale = HD ** (-0.5)

    hidden_rel = by_distance(hidden_in, me_t, tensor_n)
    grad_rel = by_distance(grad_layer_out, me_t, tensor_n)
    routes_rel = by_distance(expert_routes, me_t, tensor_n)
    row_ids = (
        ((jnp.arange(tensor_n, dtype=jnp.int32) ^ me_t) * block)[:, None]
        + jnp.arange(block, dtype=jnp.int32)[None, :]
    ).reshape(-1)

    expert_ids = jnp.arange(128, dtype=jnp.int32)
    routed = jnp.sum((routes_rel[:, :, None] == expert_ids).astype(F32), 1).astype(BF16)
    grad_own = jnp.concatenate([grad_rel, routed], 1)
    grad_sets = [gather_expert(grad_own)] + [
        gather_expert(swap(grad_own, "dp", k)) for k in range(1, dp_n)
    ]

    hidden_float = hidden_rel.astype(F32)
    first_scale = lax.rsqrt(jnp.mean(hidden_float * hidden_float, -1, keepdims=True) + EPSILON)
    first_hat = hidden_float * first_scale
    first_float = first_gain.astype(F32)
    first_normed = (first_hat * first_float).astype(BF16)
    segment, positions = positions_of(seq_lengths[0], row_ids)
    cosine_table, sine_table = rope_tables(positions, HD)
    query_pre = dot(first_normed, query_weight, ((1,), (0,))).reshape(tokens_here, query_heads, HD)
    key_pre = dot(first_normed, key_weight, ((1,), (0,))).reshape(tokens_here, kv_heads, HD)
    queries = rotate(query_pre, cosine_table, sine_table).astype(BF16)
    keys_rot = rotate(key_pre, cosine_table, sine_table).astype(BF16)
    values_low = (
        dot(first_normed, value_weight, ((1,), (0,)))
        .astype(BF16)
        .reshape(tokens_here, kv_heads, HD)
    )
    grouped = queries.reshape(tokens_here, kv_heads, group_size, HD)
    scores = (
        jnp.einsum("tkgd,ukd->kgtu", grouped, keys_rot, preferred_element_type=F32) * score_scale
    )
    allowed = (segment[:, None] == segment[None, :]) & (row_ids[None, :] <= row_ids[:, None])
    masked = jnp.where(allowed, scores, -1e30)
    top_score = jnp.max(masked, -1, keepdims=True)
    exponent = jnp.exp(masked - top_score)
    probabilities = exponent / jnp.sum(exponent, -1, keepdims=True)
    probs_low = probabilities.astype(BF16)
    attended = (
        jnp.einsum("kgtu,ukd->tkgd", probs_low, values_low, preferred_element_type=F32)
        .astype(BF16)
        .reshape(tokens_here, query_heads * HD)
    )
    attn_part = dot(attended, output_weight, ((1,), (1,)))
    attn_out = reduce_tensor(attn_part, BF16)

    residual = hidden_float[:block] + attn_out
    second_scale = lax.rsqrt(jnp.mean(residual * residual, -1, keepdims=True) + EPSILON)
    second_hat = residual * second_scale
    second_float = second_gain.astype(F32)
    second_block = (second_hat * second_float).astype(BF16)
    second_group = jnp.concatenate(gather_tensor(second_block), 0)
    second_sets = [gather_expert(second_group)] + [
        gather_expert(swap(second_group, "dp", k)) for k in range(1, dp_n)
    ]

    base = jnp.reshape(me_e * local_experts, (1,)).astype(jnp.int32)
    weights = (gate_weight, up_weight, down_weight, router_weight)
    sides = [
        expert_call(i == 0, base, second_sets[i], grad_sets[i], *weights) for i in range(dp_n)
    ]
    arrival = reduce_tensor(reduce_halves(sides[0][2], sides[0][3], BF16), BF16)
    mixed = mixed_call(sides[0][1], down_weight)
    mixed = reduce_tensor(reduce_halves(mixed[0], mixed[1], BF16), BF16)
    layer_block = (residual + mixed).astype(BF16)
    place = jnp.reshape(me_d, (1,)).astype(jnp.int32)
    grad_gate, grad_upproj, grad_down = weight_grad_call(
        place,
        second_sets,
        grad_sets,
        [s[0] for s in sides],
        [s[1] for s in sides],
        local_experts,
        units,
    )

    logits = dot(second_block, router_weight, ((1,), (0,)))
    logits = jnp.where(grad_own[:block, model_width : model_width + expert_count] > 0, logits, -1e30)
    gates_block = jnp.exp(logits - jnp.max(logits, -1, keepdims=True))
    gates_block = gates_block / jnp.sum(gates_block, -1, keepdims=True)
    grad_routed = arrival[:, :model_width]
    grad_gates = (
        arrival[:, model_width : model_width + expert_count]
        + arrival[:, model_width + expert_count : model_width + 2 * expert_count]
    )
    grad_logits = gates_block * (
        grad_gates - jnp.sum(gates_block * grad_gates, -1, keepdims=True)
    )
    grad_second = grad_routed + dot(
        grad_logits, router_weight.astype(F32), ((1,), (1,)), precision=HIGH
    )
    second_gained = grad_second * second_float
    grad_resid = grad_rel[:block].astype(F32) + second_scale * (
        second_gained - second_hat * jnp.mean(second_gained * second_hat, -1, keepdims=True)
    )
    grad_out_low = jnp.concatenate(gather_tensor(grad_resid.astype(BF16)), 0)
    grad_logits_all = jnp.concatenate(gather_tensor(grad_logits), 0)
    grad_second_gain = sum(gather_tensor(jnp.sum(grad_second * second_hat, 0)))
    grad_router = dot(second_group.astype(F32), grad_logits_all, ((0,), (0,)), precision=HIGH)

    grad_outproj = reduce_plane(dot(grad_out_low, attended, ((0,), (0,))))
    grad_attended = (
        dot(grad_out_low, output_weight, ((1,), (0,)))
        .astype(BF16)
        .reshape(tokens_here, kv_heads, group_size, HD)
    )
    grad_probs = jnp.einsum(
        "tkgd,ukd->kgtu", grad_attended, values_low, preferred_element_type=F32
    )
    grad_values = (
        jnp.einsum("kgtu,tkgd->ukd", probs_low, grad_attended, preferred_element_type=F32)
        .astype(BF16)
        .reshape(tokens_here, kv_heads * HD)
    )
    grad_scores = (
        probabilities * (grad_probs - jnp.sum(probabilities * grad_probs, -1, keepdims=True))
    ).astype(BF16)
    grad_queries = (
        jnp.einsum("kgtu,ukd->tkgd", grad_scores, keys_rot, preferred_element_type=F32)
        * score_scale
    )
    grad_keys = (
        jnp.einsum("kgtu,tkgd->ukd", grad_scores, grouped, preferred_element_type=F32)
        * score_scale
    )
    grad_query_pre = (
        rotate(grad_queries.reshape(tokens_here, query_heads, HD), cosine_table, -sine_table)
        .astype(BF16)
        .reshape(tokens_here, query_heads * HD)
    )
    grad_key_pre = (
        rotate(grad_keys, cosine_table, -sine_table)
        .astype(BF16)
        .reshape(tokens_here, kv_heads * HD)
    )
    grad_first = (
        dot(grad_query_pre, query_weight, ((1,), (1,)))
        + dot(grad_key_pre, key_weight, ((1,), (1,)))
        + dot(grad_values, value_weight, ((1,), (1,)))
    )
    grad_first_part = jnp.sum(grad_first * first_hat, 0)
    grad_first = reduce_tensor(grad_first, BF16)
    first_gained = grad_first * first_float
    hat_block = first_hat[:block]
    grad_input = grad_resid + first_scale[:block] * (
        first_gained - hat_block * jnp.mean(first_gained * hat_block, -1, keepdims=True)
    )
    last = jnp.concatenate(
        [
            dot(first_normed, grad_query_pre, ((0,), (0,))),
            dot(first_normed, grad_key_pre, ((0,), (0,))),
            dot(first_normed, grad_values, ((0,), (0,))),
            grad_router,
            grad_second_gain[:, None],
            grad_first_part[:, None],
        ],
        1,
    )
    last = reduce_plane(last)
    marks = [0]
    for w in (query_heads * HD, kv_heads * HD, kv_heads * HD, expert_count, 1, 1):
        marks.append(marks[-1] + w)
    grad_query, grad_key, grad_value, grad_router, grad_second_out, grad_first_out = (
        last[:, marks[i] : marks[i + 1]] for i in range(6)
    )
    grad_first_out = sum(gather_tensor(grad_first_out[:, 0]))

    layer_out = by_distance(jnp.concatenate(gather_tensor(layer_block), 0), me_t, tensor_n)
    grad_input = by_distance(
        jnp.concatenate(gather_tensor(grad_input.astype(BF16)), 0), me_t, tensor_n
    ).astype(F32)
    return (
        layer_out,
        grad_input,
        grad_first_out,
        grad_query,
        grad_key,
        grad_value,
        grad_outproj,
        grad_second_out[:, 0],
        grad_router,
        grad_gate,
        grad_upproj,
        grad_down,
    )


def solution(mesh):
    tokens = P(("dp", "expert"), None)
    columns = P(None, "tensor")
    experts = P("expert", None, "tensor")
    rows = P(("dp", "expert"))
    both = P(("dp", "expert"), "tensor")
    expert_grads = P("expert", "dp", "tensor")
    return jax.shard_map(
        on_device,
        mesh=mesh,
        in_specs=(tokens, tokens, tokens, P())
        + (columns,) * 4
        + (P(), P())
        + (experts,) * 3
        + (tokens,),
        out_specs=(tokens, tokens, rows)
        + (both,) * 4
        + (rows, tokens)
        + (expert_grads,) * 3,
        check_vma=False,
    )
```

```python
import functools
import math

import jax
import jax.numpy as jnp
import numpy as np
from jax import lax
from jax.experimental import pallas as pl
from jax.experimental.pallas import tpu as pltpu
from jax.sharding import PartitionSpec as P

HD = 64
EPSILON = 1e-06
F32 = jnp.float32
BF16 = jnp.bfloat16
EXTRA = 128


def dot(left, right, dims):
    return lax.dot_general(left, right, (dims, ((), ())), preferred_element_type=F32)


def rope_tables(rows):
    inverse = np.exp(np.arange(HD // 2).astype(np.float32) * np.float32(-2.0 * math.log(1e4) / HD))
    angles = np.arange(rows, dtype=np.float32)[:, None] * inverse.astype(np.float32)[None, :]
    cosine, sine = np.cos(angles), np.sin(angles)
    return (
        jnp.asarray(np.concatenate([cosine] * 4, 1), F32),
        jnp.asarray(np.concatenate([-sine, sine] * 2, 1), F32),
    )


def other_halves(values):
    width = values.shape[1]
    lane = lax.broadcasted_iota(jnp.int32, values.shape, 1)
    return jnp.where(
        lane % HD < HD // 2,
        pltpu.roll(values, width - HD // 2, 1),
        pltpu.roll(values, HD // 2, 1),
    )


def widened(table, width):
    copies = width // table.shape[1]
    return table if copies == 1 else jnp.concatenate([table] * copies, 1)


def rotate(values, cosine, sine):
    width = values.shape[1]
    return values * widened(cosine, width) + other_halves(values) * widened(sine, width)


def rotate_back(values, cosine, sine):
    width = values.shape[1]
    return values * widened(cosine, width) - other_halves(values) * widened(sine, width)


def swap(x, axis, k):
    n = lax.axis_size(axis)
    return lax.ppermute(x, axis, [(i, i ^ k) for i in range(n)])


def swap_plane(x, k_dp, k_expert):
    n = lax.axis_size("expert")
    total = n * lax.axis_size("dp")
    return lax.ppermute(x, ("dp", "expert"), [(i, i ^ (k_dp * n + k_expert)) for i in range(total)])


def bits_of(n):
    k, out = n // 2, []
    while k >= 1:
        out.append(k)
        k //= 2
    return out


def gather_sets(x, near=None):
    bits = bits_of(lax.axis_size("expert"))
    sets = []
    for k_dp in range(lax.axis_size("dp")):
        if len(bits) == 2 and k_dp:
            parts = [swap(x, "dp", k_dp), swap_plane(x, k_dp, bits[0])]
            sets.append(parts + [swap(p, "expert", bits[1]) for p in parts])
            continue
        rows = swap(x, "dp", k_dp) if k_dp else x if near is None else near
        for k in bits[:-2]:
            rows = jnp.concatenate([rows, swap(rows, "expert", k)], 0)
        parts = [rows]
        for k in bits[-2:]:
            parts = parts + [swap(p, "expert", k) for p in parts]
        sets.append(parts)
    return sets


def swap_tensor(blocks):
    n = lax.axis_size("tensor")
    return [swap(blocks[k - 1], "tensor", k) for k in range(1, n)]


def gather_tensor(x):
    return [x] + swap_tensor([x] * (lax.axis_size("tensor") - 1))


def rows_at(index, rows):
    return pl.ds(pl.multiple_of(index * rows, rows), rows)


def plain_call(kernel, name, out_shape, scratch, flops, *arrays, after=(), vmem=16):
    def whole(a):
        if a.dtype == jnp.int32 and a.size <= 64:
            return pl.BlockSpec(memory_space=pltpu.SMEM)
        return pl.BlockSpec(a.shape, lambda i: (0,) * a.ndim)

    size = sum(a.size * a.dtype.itemsize for a in list(arrays) + list(out_shape))
    count, extra = len(arrays), len(after)

    def body(*refs):
        kernel(*refs[:count], *refs[count + extra :])

    arrays = list(arrays) + list(after)
    return pl.pallas_call(
        body,
        grid=(1,),
        in_specs=[whole(a) for a in arrays[:count]] + [pl.BlockSpec(memory_space=pl.ANY)] * extra,
        out_specs=[whole(a) for a in out_shape],
        out_shape=out_shape,
        scratch_shapes=scratch,
        compiler_params=pltpu.CompilerParams(vmem_limit_bytes=vmem * 2**20),
        cost_estimate=pl.CostEstimate(flops=flops, bytes_accessed=size, transcendentals=0),
        name=name,
    )(*arrays)


def array(shape, dtype):
    return jax.ShapeDtypeStruct(shape, dtype)


def spread_blocks(me, value_ref, own_ref, sent_refs):
    rows = own_ref.shape[0]
    own_ref[...] = value_ref[rows_at(me, rows), :]
    for k, ref in enumerate(sent_refs, 1):
        ref[...] = value_ref[rows_at(me ^ k, rows), :].astype(ref.dtype)


def block_shapes(block, width, n):
    return [array((block, width), F32)] + [array((block, width), BF16)] * (n - 1)


def unit_rows(values):
    return lax.rsqrt(jnp.mean(values * values, -1, keepdims=True) + EPSILON)


def attend_kernel(heads, group, *refs):
    (meta, lengths, hidden, gain, query_w, key_w, value_w, output_w, cosine, sine) = refs[:10]
    n1_ref, qkv_ref, prob_ref, att_ref, cos_ref, sin_ref = refs[10:16]
    own_ref, *sent_refs = refs[16:-1]
    part_scr = refs[-1]
    x = hidden[...].astype(F32)
    n1 = (x * unit_rows(x) * gain[0:1, :]).astype(BF16)
    n1_ref[...] = n1
    tokens = x.shape[0]
    rows = lax.broadcasted_iota(jnp.int32, (tokens, tokens), 0)
    columns = lax.broadcasted_iota(jnp.int32, (tokens, tokens), 1)
    table_rows = lax.broadcasted_iota(jnp.int32, cosine.shape, 0)
    cos, sin = cosine[...], sine[...]
    row_segment, column_segment = jnp.zeros_like(rows), jnp.zeros_like(rows)
    end = 0
    for i in range(lengths.shape[1] - 1):
        end = end + lengths[0, i]
        row_segment += (rows >= end).astype(jnp.int32)
        column_segment += (columns >= end).astype(jnp.int32)
        cos = jnp.where(table_rows >= end, pltpu.roll(cosine[...], end, 0), cos)
        sin = jnp.where(table_rows >= end, pltpu.roll(sine[...], end, 0), sin)
    cos_ref[...] = cos
    sin_ref[...] = sin
    allowed = (row_segment == column_segment) & (columns <= rows)
    q_width, kv_width = query_w.shape[1], key_w.shape[1]
    keys_at, values_at = q_width, q_width + kv_width
    qkv_ref[:, :q_width] = rotate(dot(n1, query_w[...], ((1,), (0,))), cos, sin).astype(BF16)
    qkv_ref[:, keys_at:values_at] = rotate(dot(n1, key_w[...], ((1,), (0,))), cos, sin).astype(BF16)
    qkv_ref[:, values_at:] = dot(n1, value_w[...], ((1,), (0,))).astype(BF16)
    for h in range(heads):
        g = h // group
        scores = dot(
            qkv_ref[:, h * HD : (h + 1) * HD],
            qkv_ref[:, keys_at + g * HD : keys_at + (g + 1) * HD],
            ((1,), (1,)),
        )
        masked = jnp.where(allowed, scores * HD ** (-0.5), -1e30)
        exponent = jnp.exp(masked - jnp.max(masked, -1, keepdims=True))
        prob = exponent / jnp.sum(exponent, -1, keepdims=True)
        prob_ref[h] = prob
        head_out = dot(
            prob.astype(BF16), qkv_ref[:, values_at + g * HD : values_at + (g + 1) * HD], ((1,), (0,))
        )
        att_ref[:, h * HD : (h + 1) * HD] = head_out.astype(BF16)
    part_scr[...] = dot(att_ref[...], output_w[...], ((1,), (1,)))
    spread_blocks(meta[0], part_scr, own_ref, sent_refs)
    own_ref[...] += hidden[rows_at(meta[0], own_ref.shape[0]), :].astype(F32)


def routes_kernel(routes, dy, out_ref):
    width = dy.shape[1]
    out_ref[:, :width] = dy[...]
    named = routes[...].astype(F32).T
    lane = lax.broadcasted_iota(jnp.int32, (dy.shape[0], EXTRA), 1).astype(F32)
    total = jnp.zeros(lane.shape, F32)
    for j in range(named.shape[1]):
        total += (named[:, j : j + 1] == lane).astype(F32)
    out_ref[:, width:] = total.astype(BF16)


def second_norm_kernel(gain, grad, *refs):
    parts, (residual_ref, n2_ref, grad_ref) = refs[:-3], refs[-3:]
    residual = parts[0][...]
    for part in parts[1:]:
        residual = residual + part[...].astype(F32)
    residual_ref[...] = residual
    n2_ref[...] = (residual * unit_rows(residual) * gain[1:2, :]).astype(BF16)
    grad_ref[...] = grad[...]


def place_kernel(meta, *refs):
    blocks, out_ref = refs[:-1], refs[-1]
    rows = blocks[0].shape[0]
    for k, ref in enumerate(blocks):
        out_ref[rows_at(meta[0] ^ k, rows), :] = ref[...].astype(out_ref.dtype)


def halves_kernel(meta, near, got, last, *refs):
    own_ref, *sent_refs = refs[:-1]
    total_scr = refs[-1]
    rows = last.shape[0]
    total_scr[...] = (
        near[:rows, :].astype(F32) + got[:rows, :].astype(F32) + last[...].astype(F32)
    )
    spread_blocks(meta[0], total_scr, own_ref, sent_refs)


def residual_grad_kernel(experts, tensor_n, meta, residual_ref, n2_ref, dy_ref, router, gain, *refs):
    mixed_near, mixed_got, mixed_last = refs[:3]
    parts, refs = refs[3 : 3 + tensor_n], refs[3 + tensor_n :]
    dh_ref, gain_row_ref, message_ref, mixed_ref, *sent_refs = refs[:-1]
    mixed_scr = refs[-1]
    tokens = dy_ref.shape[0]
    mixed_scr[...] = (
        mixed_near[:tokens, :].astype(F32)
        + mixed_got[:tokens, :].astype(F32)
        + mixed_last[...].astype(F32)
    )
    block, width = residual_ref.shape
    mine = rows_at(meta[0], block)
    arrival = parts[0][...]
    for part in parts[1:]:
        arrival = arrival + part[...].astype(F32)
    logits = dot(n2_ref[...], router[...], ((1,), (1,)))
    routed = dy_ref[mine, width : width + experts].astype(F32) > 0.5
    logits = jnp.where(routed, logits, -1e30)
    gates = jnp.exp(logits - jnp.max(logits, -1, keepdims=True))
    gates = gates / jnp.sum(gates, -1, keepdims=True)
    extra = arrival[:, width:]
    dg = extra[:, :experts] + pltpu.roll(extra, EXTRA - experts, 1)[:, :experts]
    dlog = gates * (dg - jnp.sum(gates * dg, -1, keepdims=True))
    high = dlog.astype(BF16)
    low = (dlog - high.astype(F32)).astype(BF16)
    dn2 = (
        arrival[:, :width]
        + dot(high, router[...], ((1,), (0,)))
        + dot(low, router[...], ((1,), (0,)))
    )
    residual = residual_ref[...]
    scale = unit_rows(residual)
    hat = residual * scale
    gain_row_ref[...] = jnp.zeros_like(gain_row_ref)
    gain_row_ref[0:1, :] = jnp.sum(dn2 * hat, 0, keepdims=True)
    gained = dn2 * gain[1:2, :]
    dh = dy_ref[mine, :width].astype(F32) + scale * (
        gained - hat * jnp.mean(gained * hat, -1, keepdims=True)
    )
    dh_ref[...] = dh
    message_ref[:, :width] = dh.astype(BF16)
    message_ref[:, width:] = jnp.zeros((block, EXTRA), BF16)
    message_ref[:, width : width + experts] = high
    message_ref[:, width + experts : width + 2 * experts] = low
    mixed_ref[...] = mixed_scr[mine, :]
    for k, ref in enumerate(sent_refs, 1):
        ref[:, : width + EXTRA] = message_ref[...]
        ref[:, width + EXTRA :] = mixed_scr[rows_at(meta[0] ^ k, block), :].astype(BF16)


def attend_grad_kernel(heads, group, experts, expert_n, dp_n, tensor_n, *refs):
    (meta, hidden, gain_row, n1_ref, n2_ref, qkv_ref, prob_ref, att_ref, cos_ref, sin_ref) = refs[:10]
    query_w, key_w, value_w, output_w = refs[10:14]
    messages = refs[14 : 14 + tensor_n]
    mixed_own, residual_ref = refs[14 + tensor_n : 16 + tensor_n]
    near_ref, far_ref, layer_ref, own_ref, *sent_refs = refs[16 + tensor_n : -6]
    dh_scr, dqkv_scr, raw_scr, dn1_scr, left_scr, side_scr = refs[-6:]
    block = messages[0].shape[0]
    width = hidden.shape[1]
    for k, ref in enumerate(messages):
        dh_scr[rows_at(meta[0] ^ k, block), :] = ref[:, : width + EXTRA]
    cos, sin = cos_ref[...], sin_ref[...]
    q_width, kv_width = query_w.shape[1], key_w.shape[1]
    keys_at, values_at = q_width, q_width + kv_width
    dob = dh_scr[:, :width]
    da = dot(dob, output_w[...], ((1,), (0,))).astype(BF16)
    scale = HD ** (-0.5)
    for g in range(heads // group):
        key = qkv_ref[:, keys_at + g * HD : keys_at + (g + 1) * HD]
        value = qkv_ref[:, values_at + g * HD : values_at + (g + 1) * HD]
        dk = dv = 0.0
        for h in range(g * group, (g + 1) * group):
            da_h = da[:, h * HD : (h + 1) * HD]
            prob = prob_ref[h]
            dprob = dot(da_h, value, ((1,), (1,)))
            ds = prob * (dprob - jnp.sum(prob * dprob, -1, keepdims=True))
            raw_scr[:, h * HD : (h + 1) * HD] = dot(ds.astype(BF16), key, ((1,), (0,))) * scale
            dk = dk + dot(ds.T.astype(BF16), qkv_ref[:, h * HD : (h + 1) * HD], ((1,), (0,)))
            dv = dv + dot(prob.T.astype(BF16), da_h, ((1,), (0,)))
        raw_scr[:, keys_at + g * HD : keys_at + (g + 1) * HD] = dk * scale
        dqkv_scr[:, values_at + g * HD : values_at + (g + 1) * HD] = dv.astype(BF16)
    dqkv_scr[:, :q_width] = rotate_back(raw_scr[:, :q_width], cos, sin).astype(BF16)
    dqkv_scr[:, keys_at:values_at] = rotate_back(raw_scr[:, keys_at:values_at], cos, sin).astype(BF16)
    dn1 = (
        dot(dqkv_scr[:, :q_width], query_w[...], ((1,), (1,)))
        + dot(dqkv_scr[:, keys_at:values_at], key_w[...], ((1,), (1,)))
        + dot(dqkv_scr[:, values_at:], value_w[...], ((1,), (1,)))
    )
    dn1_scr[...] = dn1
    layer = residual_ref[...] + mixed_own[...]
    for ref in messages[1:]:
        layer = layer + ref[:, width + EXTRA :].astype(F32)
    layer_ref[...] = layer.astype(BF16)
    own_ref[...] = dn1_scr[rows_at(meta[0], block), :]
    for k, ref in enumerate(sent_refs, 1):
        ref[:, :width] = dn1_scr[rows_at(meta[0] ^ k, block), :].astype(BF16)
        ref[:, width:] = layer.astype(BF16)
    x = hidden[...].astype(F32)
    first_row = jnp.sum(dn1 * (x * unit_rows(x)), 0, keepdims=True)
    dlog_t = dh_scr[:, width:].astype(F32).T.astype(BF16)
    router_t = dot(dlog_t, n2_ref[...], ((1,), (0,)))
    router_t = router_t[:experts] + router_t[experts : 2 * experts]
    side = jnp.concatenate(
        [router_t, gain_row[0:1, :], first_row, jnp.zeros((EXTRA - experts - 2, width), F32)], 0
    )
    side_scr[...] = side.T.astype(BF16)
    left_scr[:width, :] = n1_ref[...].T
    left_scr[width:, :] = dob.T
    places = expert_n * dp_n
    rows = width // places
    expert_bits = list(reversed(bits_of(expert_n)))
    qkv_width = values_at + kv_width
    for at in range(places):
        bits = [(at // (places >> (i + 1))) % 2 for i in range(len(expert_bits))]
        e_rel = sum(b * k for b, k in zip(bits, expert_bits))
        index = (meta[2] ^ (at % dp_n)) * expert_n + (meta[1] ^ e_rel)
        out = near_ref if at < places // 2 else far_ref
        to = slice((at % (places // 2)) * rows, (at % (places // 2) + 1) * rows)
        source = rows_at(index, rows)
        out[to, :qkv_width] = dot(left_scr[source, :], dqkv_scr[...], ((1,), (0,))).astype(BF16)
        out[to, qkv_width : qkv_width + EXTRA] = side_scr[source, :]
        below = left_scr[rows_at(index + places, rows), :]
        out[to, qkv_width + EXTRA :] = dot(below, att_ref[...], ((1,), (0,))).astype(BF16)


def input_grad_kernel(meta, hidden, gain, dh_ref, gains_ref, *refs):
    parts, out_ref = refs[:-1], refs[-1]
    block, width = dh_ref.shape
    dn1 = parts[0][...]
    for part in parts[1:]:
        dn1 = dn1 + part[:, :width].astype(F32)
    x = hidden[rows_at(meta[0], block), :].astype(F32)
    scale = unit_rows(x)
    hat = x * scale
    gained = dn1 * gain[0:1, :]
    grad = dh_ref[...] + scale * (gained - hat * jnp.mean(gained * hat, -1, keepdims=True))
    out_ref[:, :width] = grad.astype(BF16)
    rows, columns = gains_ref.shape
    gains = gains_ref[...]
    high = gains.astype(BF16).astype(F32)
    out_ref[:, width:] = jnp.zeros((block, EXTRA), BF16)
    out_ref[: 2 * rows, width : width + columns] = jnp.concatenate(
        [high, gains - high], 0
    ).astype(BF16)


def place_last_kernel(tensor_n, meta, layer_own, *refs):
    layers, blocks = refs[: tensor_n - 1], refs[tensor_n - 1 : -4]
    layer_ref, grad_ref, first_ref, second_ref = refs[-4:]
    rows, width = layer_own.shape
    layer_ref[rows_at(meta[0], rows), :] = layer_own[...]
    for k, ref in enumerate(layers, 1):
        layer_ref[rows_at(meta[0] ^ k, rows), :] = ref[:, width:]
    gains = 0.0
    for k, ref in enumerate(blocks):
        grad_ref[rows_at(meta[0] ^ k, rows), :] = ref[:, :width].astype(F32)
        gains = gains + ref[:16, width:].astype(F32)
    gains = gains[:8] + gains[8:]
    columns = first_ref.shape[1]
    second_ref[...] = gains[0:1, :columns]
    first_ref[...] = gains[1:2, :columns]


def half_kernel(near, got, out_ref):
    half = out_ref.shape[0]
    out_ref[...] = (near[half:, :].astype(F32) + got[half:, :].astype(F32)).astype(BF16)


def add_kernel(near, got, own_ref, *sent_refs):
    rows = own_ref.shape[0]
    for k, ref in enumerate([own_ref] + list(sent_refs)):
        at = slice(k * rows, (k + 1) * rows)
        ref[...] = (near[at, :].astype(F32) + got[at, :].astype(F32)).astype(ref.dtype)


def last_kernel(experts, q_width, kv_width, *refs):
    parts, outs = refs[:-6], refs[-6:]
    total = parts[0][...]
    for part in parts[1:]:
        total = total + part[...].astype(F32)
    at = 0
    for ref, width in zip(outs[:3], (q_width, kv_width, kv_width)):
        ref[...] = total[:, at : at + width]
        at += width
    side = total[:, at : at + EXTRA]
    outs[3][...] = total[:, at + EXTRA :]
    side = side.T
    outs[4][...] = side[:experts]
    outs[5][...] = side[experts : experts + 8]


def pair_of(local_experts):
    return 2 if local_experts % 2 == 0 else 1


def kernel_params(tokens, vmem=28):
    return pltpu.CompilerParams(vmem_limit_bytes=(vmem if tokens <= 512 else 60) * 2**20)


def side_by_side(ref, first, count):
    parts = [ref[first + i] for i in range(count)]
    return parts[0] if count == 1 else jnp.concatenate(parts, 1)


def split_rows(chunk, chunks, value, near_ref, far_ref):
    if chunks == 1:
        half = value.shape[0] // 2
        near_ref[...] = value[:half]
        far_ref[...] = value[half:]
        return
    rows = value.shape[0]

    @pl.when(chunk < chunks // 2)
    def _():
        near_ref[pl.ds(pl.multiple_of(chunk * rows, rows), rows), :] = value

    @pl.when(chunk >= chunks // 2)
    def _():
        at = (chunk - chunks // 2) * rows
        far_ref[pl.ds(pl.multiple_of(at, rows), rows), :] = value


def expert_kernel(own, steps, pair, experts, parts, extra, *refs):
    meta_ref, refs = refs[0], refs[1:]
    x_parts, dy_parts, refs = refs[:parts], refs[parts : 2 * parts], refs[2 * parts :]
    gate_ref, up_ref, down_ref, router_ref = refs[:4]
    refs = refs[extra:]
    both_ref, gated_ref = refs[4:6]
    if own:
        dg_ref, dg_scr = refs[6], refs[-1]
        refs = refs[7:-1]
    else:
        refs = refs[6:]
    gates_scr, x_ref, dy_ref = refs
    step = pl.program_id(1)
    width = x_ref.shape[1]
    lanes = gates_scr.shape[1]

    @pl.when(step == 0)
    def _():
        part_rows = x_parts[0].shape[0]
        for n in range(parts):
            x_ref[n * part_rows : (n + 1) * part_rows, :] = x_parts[n][...]
            dy_ref[n * part_rows : (n + 1) * part_rows, :] = dy_parts[n][...]
        logits = dot(x_ref[...], router_ref[...], ((1,), (1,)))
        routed = dy_ref[:, width : width + experts].astype(F32) > 0.5
        logits = jnp.where(routed, logits, -1e30)
        weights = jnp.exp(logits - jnp.max(logits, -1, keepdims=True))
        gates_scr[...] = jnp.zeros_like(gates_scr)
        gates_scr[:, :experts] = weights / jnp.sum(weights, -1, keepdims=True)
        if own:
            dg_scr[...] = jnp.zeros_like(dg_scr)

    first = meta_ref[1] * (pair * steps) + step * pair
    gates = pltpu.roll(gates_scr[...], lax.rem(lanes - first, lanes), 1)
    raw_all = dot(dy_ref[:, :width], side_by_side(down_ref, 0, pair), ((1,), (0,)))
    units = gate_ref.shape[2]
    column = lax.broadcasted_iota(jnp.int32, gates.shape, 1)
    weight = jnp.concatenate([r[i] for i in range(pair) for r in (gate_ref, up_ref)], 1)
    both_all = dot(x_ref[...], weight, ((1,), (0,)))
    for i in range(pair):
        gate_proj = both_all[:, 2 * i * units : (2 * i + 1) * units]
        up_proj = both_all[:, (2 * i + 1) * units : (2 * i + 2) * units]
        raw = raw_all[:, i * units : (i + 1) * units]
        mine = gates[:, i : i + 1]
        sigmoid_gate = 0.5 * jnp.tanh(0.5 * gate_proj) + 0.5
        activated = gate_proj * sigmoid_gate
        hidden = activated * up_proj
        grad_hidden = raw * mine
        grad_gate = grad_hidden * up_proj * (sigmoid_gate + activated * (1.0 - sigmoid_gate))
        at = 2 * i * units
        both_ref[:, at : at + units] = grad_gate.astype(BF16)
        both_ref[:, at + units : at + 2 * units] = (grad_hidden * activated).astype(BF16)
        gated_ref[:, i * units : (i + 1) * units] = (hidden * mine).astype(BF16)
        if own:
            dg = jnp.sum(raw * hidden, 1, keepdims=True)
            dg_scr[...] += jnp.where(column == first + i, dg, 0.0)
    if own:

        @pl.when(step == steps - 1)
        def _():
            dg = dg_scr[...]
            high = dg.astype(BF16).astype(F32)
            low = pltpu.roll(dg - high, experts, 1)
            dg_ref[...] = (high + low).astype(BF16)


def expert_call(own, meta, xs, dys, gate_weight, up_weight, down_weight, router_weight, after=()):
    part_rows, width = xs[0].shape
    parts = len(xs)
    tokens = part_rows * parts
    if tokens > 512:
        xs, dys, parts = [jnp.concatenate(xs, 0)], [jnp.concatenate(dys, 0)], 1
        part_rows = tokens
    dy_width = dys[0].shape[1]
    local, _, units = gate_weight.shape
    experts = router_weight.shape[0]
    pair = pair_of(local)
    rows = min(tokens, 512)
    chunks, steps = tokens // rows, local // pair
    grid_spec = dict(
        grid=(chunks, steps),
        in_specs=[
            pl.BlockSpec(memory_space=pltpu.SMEM),
        ]
        + [pl.BlockSpec((rows // parts, width), lambda c, s: (c, 0))] * parts
        + [pl.BlockSpec((rows // parts, dy_width), lambda c, s: (c, 0))] * parts
        + [pl.BlockSpec((pair, width, units), lambda c, s: (s, 0, 0))] * 3
        + [pl.BlockSpec(router_weight.shape, lambda c, s: (0, 0))]
        + [pl.BlockSpec(memory_space=pl.ANY)] * len(after),
        out_specs=[
            pl.BlockSpec((rows, pair * 2 * units), lambda c, s: (c, s)),
            pl.BlockSpec((rows, pair * units), lambda c, s: (c, s)),
        ],
        scratch_shapes=[
            pltpu.VMEM((rows, 128), F32),
            pltpu.VMEM((rows, width), BF16),
            pltpu.VMEM((rows, dy_width), BF16),
        ],
    )
    out_shape = [
        jax.ShapeDtypeStruct((tokens, local * 2 * units), BF16),
        jax.ShapeDtypeStruct((tokens, local * units), BF16),
    ]
    if own:
        grid_spec["out_specs"] += [pl.BlockSpec((rows, EXTRA), lambda c, s: (c, 0))]
        out_shape += [jax.ShapeDtypeStruct((tokens, EXTRA), BF16)]
        grid_spec["scratch_shapes"] += [pltpu.VMEM((rows, 128), F32)]
    products = 3
    return pl.pallas_call(
        functools.partial(expert_kernel, own, steps, pair, experts, parts, len(after)),
        out_shape=out_shape,
        compiler_params=kernel_params(tokens),
        cost_estimate=pl.CostEstimate(
            flops=2 * products * tokens * width * local * units,
            bytes_accessed=2 * (3 * local * width * units + 3 * tokens * width),
            transcendentals=tokens * local * units,
        ),
        name="experts_own" if own else "experts_far",
        **grid_spec,
    )(meta, *xs, *dys, gate_weight, up_weight, down_weight, router_weight, *after)


def arrival_kernel(chunks, steps, pair, both_ref, dg_ref, gate_ref, up_ref, *refs):
    near_ref, far_ref, total_scr = refs[-3:]
    chunk, step = pl.program_id(0), pl.program_id(1)

    @pl.when(step == 0)
    def _():
        total_scr[...] = jnp.zeros_like(total_scr)

    weight = jnp.concatenate([r[i] for i in range(pair) for r in (gate_ref, up_ref)], 1)
    total_scr[...] += dot(both_ref[...], weight, ((1,), (1,)))

    @pl.when(step == steps - 1)
    def _():
        message = jnp.concatenate([total_scr[...].astype(BF16), dg_ref[...]], 1)
        split_rows(chunk, chunks, message, near_ref, far_ref)


def arrival_call(both, dg, gate_weight, up_weight, after=()):
    tokens = both.shape[0]
    local, width, units = gate_weight.shape
    pair = pair_of(local)
    rows = min(tokens, 512)
    chunks, steps = tokens // rows, local // pair
    half = (tokens // 2, width + EXTRA)
    return pl.pallas_call(
        functools.partial(arrival_kernel, chunks, steps, pair),
        grid=(chunks, steps),
        in_specs=[
            pl.BlockSpec((rows, pair * 2 * units), lambda c, s: (c, s)),
            pl.BlockSpec((rows, EXTRA), lambda c, s: (c, 0)),
        ]
        + [pl.BlockSpec((pair, width, units), lambda c, s: (s, 0, 0))] * 2
        + [pl.BlockSpec(memory_space=pl.ANY)] * len(after),
        out_specs=[pl.BlockSpec(half, lambda c, s: (0, 0))] * 2,
        out_shape=[jax.ShapeDtypeStruct(half, BF16)] * 2,
        scratch_shapes=[pltpu.VMEM((rows, width), F32)],
        compiler_params=kernel_params(tokens),
        cost_estimate=pl.CostEstimate(
            flops=4 * tokens * width * local * units,
            bytes_accessed=4 * (local * width * units + 2 * tokens * width),
            transcendentals=0,
        ),
        name="experts_arrival",
    )(both, dg, gate_weight, up_weight, *after)


def mixed_kernel(chunks, steps, pair, gated_ref, down_ref, *refs):
    near_ref, far_ref, total_scr = refs[-3:]
    chunk, step = pl.program_id(0), pl.program_id(1)

    @pl.when(step == 0)
    def _():
        total_scr[...] = jnp.zeros_like(total_scr)

    total_scr[...] += dot(gated_ref[...], side_by_side(down_ref, 0, pair), ((1,), (1,)))

    @pl.when(step == steps - 1)
    def _():
        split_rows(chunk, chunks, total_scr[...].astype(BF16), near_ref, far_ref)


def mixed_call(gated, down_weight, after=()):
    tokens = gated.shape[0]
    local, width, units = down_weight.shape
    pair = pair_of(local)
    rows = min(tokens, 512)
    chunks, steps = tokens // rows, local // pair
    half = (tokens // 2, width)
    return pl.pallas_call(
        functools.partial(mixed_kernel, chunks, steps, pair),
        grid=(chunks, steps),
        in_specs=[
            pl.BlockSpec((rows, pair * units), lambda c, s: (c, s)),
            pl.BlockSpec((pair, width, units), lambda c, s: (s, 0, 0)),
        ]
        + [pl.BlockSpec(memory_space=pl.ANY)] * len(after),
        out_specs=[pl.BlockSpec(half, lambda c, s: (0, 0))] * 2,
        out_shape=[jax.ShapeDtypeStruct(half, BF16)] * 2,
        scratch_shapes=[pltpu.VMEM((rows, width), F32)],
        compiler_params=kernel_params(tokens),
        cost_estimate=pl.CostEstimate(
            flops=2 * tokens * width * local * units,
            bytes_accessed=2 * (local * width * units + 2 * tokens * width),
            transcendentals=0,
        ),
        name="experts_mixed",
    )(gated, down_weight, *after)


def weight_grad_kernel(sets, parts, outs, pair, units, place_ref, *refs):
    lefts, rights = refs[: sets * parts], refs[sets * parts : sets * parts + sets]
    grad_refs, left_scr = refs[-1 - outs : -1], refs[-1]

    @pl.when(pl.program_id(0) == 0)
    def _():
        for n in range(sets * parts):
            rows = lefts[n].shape[0]
            left_scr[:, n * rows : (n + 1) * rows] = lefts[n][...].T

    rows = rights[0].shape[0]
    total = None
    for n in range(sets):
        part = dot(left_scr[:, n * rows : (n + 1) * rows], rights[n][...], ((1,), (0,)))
        total = part if total is None else total + part
    for i in range(pair):
        for j in range(outs):
            at = (i * outs + j) * units
            grad_refs[j][i] = total[:, at : at + units]


def weight_grad_call(meta, lefts, rights, local, units, after=()):
    sets, parts = len(lefts), len(lefts[0])
    outs = rights[0].shape[1] // (local * units)
    part_rows = lefts[0][0].shape[0]
    width = lefts[0][0].shape[1] // 128 // sets * 128
    tokens = part_rows * parts
    lefts = sum(lefts, [])
    pair = pair_of(local)
    columns = pl.BlockSpec(
        (part_rows, width), lambda s, meta: (0, meta[2]), pipeline_mode=pl.Buffered(1)
    )
    return pl.pallas_call(
        functools.partial(weight_grad_kernel, sets, parts, outs, pair, units),
        grid_spec=pltpu.PrefetchScalarGridSpec(
            num_scalar_prefetch=1,
            grid=(local // pair,),
            in_specs=[columns] * (sets * parts)
            + [pl.BlockSpec((tokens, pair * outs * units), lambda s, meta: (0, s))] * sets
            + [pl.BlockSpec(memory_space=pl.ANY)] * len(after),
            out_specs=[pl.BlockSpec((pair, width, units), lambda s, meta: (s, 0, 0))] * outs,
            scratch_shapes=[pltpu.VMEM((width, sets * tokens), BF16)],
        ),
        out_shape=[jax.ShapeDtypeStruct((local, width, units), F32)] * outs,
        compiler_params=kernel_params(tokens),
        cost_estimate=pl.CostEstimate(
            flops=2 * sets * tokens * width * outs * local * units,
            bytes_accessed=4 * outs * local * width * units + 4 * sets * tokens * width,
            transcendentals=0,
        ),
        name="experts_weight_grads",
    )(meta, *lefts, *rights, *after)


def reduce_first(near, far, after=()):
    bits = list(reversed(bits_of(lax.axis_size("expert"))))
    for k in bits[:-2]:
        got = swap(far, "expert", k)
        total = (near.astype(F32) + got.astype(F32)).astype(BF16)
        near, far = jnp.split(total, 2, 0)
    got = swap(far, "expert", bits[-2])
    half = near.shape[0] // 2
    if after:
        (sent,) = plain_call(
            half_kernel,
            "half",
            [array((half, near.shape[1]), BF16)],
            [],
            near.size,
            near,
            got,
            after=after,
        )
    else:
        sent = (near[half:].astype(F32) + got[half:].astype(F32)).astype(BF16)
    return near, got, swap(sent, "expert", bits[-1])


def on_device(
    hidden_in,
    seq_lengths,
    expert_routes,
    first_gain,
    query_weight,
    key_weight,
    value_weight,
    output_weight,
    second_gain,
    router_weight,
    gate_weight,
    up_weight,
    down_weight,
    grad_layer_out,
):
    tokens_here, model_width = hidden_in.shape
    q_width, kv_width = query_weight.shape[1], key_weight.shape[1]
    heads, group = q_width // HD, q_width // kv_width
    expert_count = router_weight.shape[1]
    local_experts, _, units = gate_weight.shape
    tensor_n = lax.axis_size("tensor")
    expert_n = lax.axis_size("expert")
    dp_n = lax.axis_size("dp")
    block = tokens_here // tensor_n
    meta = jnp.stack([lax.axis_index(a) for a in ("tensor", "expert", "dp")]).astype(jnp.int32)
    gain_rows = jnp.stack([first_gain, second_gain]).astype(F32)

    (grad_own,) = plain_call(
        routes_kernel,
        "routes",
        [array((tokens_here, model_width + EXTRA), BF16)],
        [],
        tokens_here * model_width,
        expert_routes.T,
        grad_layer_out,
        vmem=60,
    )

    cosine, sine = rope_tables(tokens_here)
    blocks = block_shapes(block, model_width, tensor_n)
    n1, qkv, prob, att, cosine, sine, part, *sent = plain_call(
        functools.partial(attend_kernel, heads, group),
        "attend",
        [
            array((tokens_here, model_width), BF16),
            array((tokens_here, q_width + 2 * kv_width), BF16),
            array((heads, tokens_here, tokens_here), F32),
            array((tokens_here, q_width), BF16),
            array(cosine.shape, F32),
            array(sine.shape, F32),
        ]
        + blocks,
        [pltpu.VMEM((tokens_here, model_width), F32)],
        2 * tokens_here * model_width * 3 * q_width,
        meta,
        seq_lengths,
        hidden_in,
        gain_rows,
        query_weight,
        key_weight,
        value_weight,
        output_weight,
        cosine,
        sine,
        vmem=60,
    )
    far_grads = [swap(grad_own, "dp", k) for k in range(1, dp_n)]
    if expert_n == 4:
        far_grads += [swap_plane(grad_own, k, 2) for k in range(1, dp_n)]
    residual, second_block, grad_near = plain_call(
        second_norm_kernel,
        "second_norm",
        [
            array((block, model_width), F32),
            array((block, model_width), BF16),
            array(grad_own.shape, BF16),
        ],
        [],
        8 * block * model_width,
        gain_rows,
        grad_own,
        part,
        *swap_tensor(sent),
        after=far_grads,
    )
    grad_sets = gather_sets(grad_own, grad_near)
    (second_group,) = plain_call(
        place_kernel,
        "place_second",
        [array((tokens_here, model_width), BF16)],
        [],
        tokens_here * model_width,
        meta,
        *gather_tensor(second_block),
        after=grad_sets[0][1:2],
    )
    second_sets = gather_sets(second_group)

    router_t = router_weight.T
    weights = (gate_weight, up_weight, down_weight, router_t)
    far_grads = [g for x in grad_sets[1:] for g in x[2:]]
    own = expert_call(True, meta, second_sets[0], grad_sets[0], *weights, after=far_grads)
    arrival = arrival_call(
        own[0], own[2], gate_weight, up_weight, after=[x for y in second_sets[1:] for x in y[:2]]
    )
    sides = [own] + [
        expert_call(False, meta, second_sets[i], grad_sets[i], *weights) for i in range(1, dp_n)
    ]
    mixed = mixed_call(own[1], down_weight, after=arrival[:1])
    arrival = plain_call(
        halves_kernel,
        "arrival_blocks",
        block_shapes(block, model_width + EXTRA, tensor_n),
        [pltpu.VMEM((tokens_here, model_width + EXTRA), F32)],
        2 * tokens_here * model_width,
        meta,
        *reduce_first(*arrival),
        after=[mixed[0]] + [x[1] for x in sides[1:]],
    )
    mixed = reduce_first(*mixed, after=arrival[:1])
    arrival = [arrival[0]] + swap_tensor(arrival[1:])
    (grad_down,) = weight_grad_call(
        meta, grad_sets, [x[1] for x in sides], local_experts, units
    )
    grad_gate, grad_upproj = weight_grad_call(
        meta, second_sets, [x[0] for x in sides], local_experts, units
    )

    grad_resid, gain_row, message, mixed_own, *sent = plain_call(
        functools.partial(residual_grad_kernel, expert_count, tensor_n),
        "residual_grad",
        [
            array((block, model_width), F32),
            array((8, model_width), F32),
            array((block, model_width + EXTRA), BF16),
            array((block, model_width), F32),
        ]
        + [array((block, 2 * model_width + EXTRA), BF16)] * (tensor_n - 1),
        [pltpu.VMEM((tokens_here, model_width), F32)],
        20 * block * model_width,
        meta,
        residual,
        second_block,
        grad_own,
        router_t,
        gain_rows,
        *mixed,
        *arrival,
        after=[grad_down],
    )
    places = expert_n * dp_n
    rows = model_width // places
    last_width = 2 * q_width + 2 * kv_width + EXTRA
    near, far, layer_block, *dn1 = plain_call(
        functools.partial(
            attend_grad_kernel, heads, group, expert_count, expert_n, dp_n, tensor_n
        ),
        "attend_grad",
        [array((model_width // 2, last_width), BF16)] * 2
        + [array((block, model_width), BF16), array((block, model_width), F32)]
        + [array((block, 2 * model_width), BF16)] * (tensor_n - 1),
        [
            pltpu.VMEM((tokens_here, model_width + EXTRA), BF16),
            pltpu.VMEM((tokens_here, q_width + 2 * kv_width), BF16),
            pltpu.VMEM((tokens_here, q_width + kv_width), F32),
            pltpu.VMEM((tokens_here, model_width), F32),
            pltpu.VMEM((2 * model_width, tokens_here), BF16),
            pltpu.VMEM((model_width, EXTRA), BF16),
        ],
        2 * tokens_here * model_width * 6 * q_width,
        meta,
        hidden_in,
        gain_row,
        n1,
        second_group,
        qkv,
        prob,
        att,
        cosine,
        sine,
        query_weight,
        key_weight,
        value_weight,
        output_weight,
        message,
        *swap_tensor(sent),
        mixed_own,
        residual,
        after=[grad_gate],
    )

    expert_bits = list(reversed(bits_of(expert_n)))
    for k in expert_bits[:-2]:
        total = near.astype(F32) + swap(far, "expert", k).astype(F32)
        near, far = jnp.split(total.astype(BF16), 2, 0)
    got = swap(far, "expert", expert_bits[-2])
    shapes = [array((rows, last_width), F32)] + [array((rows, last_width), BF16)] * (2 * dp_n - 1)
    own_rows, *sent = plain_call(
        add_kernel, "plane_add", shapes, [], model_width * last_width, near, got
    )
    ways = [(k % dp_n, (k // dp_n) * expert_bits[-1]) for k in range(1, 2 * dp_n)]
    got = [swap_plane(x, *way) for x, way in zip(sent, ways)]
    grad_query, grad_key, grad_value, grad_outproj, grad_router, gains = plain_call(
        functools.partial(last_kernel, expert_count, q_width, kv_width),
        "plane_last",
        [
            array((rows, q_width), F32),
            array((rows, kv_width), F32),
            array((rows, kv_width), F32),
            array((rows, q_width), F32),
            array((expert_count, rows), F32),
            array((8, rows), F32),
        ],
        [],
        4 * rows * last_width,
        own_rows,
        *got,
    )
    dn1 = [dn1[0]] + swap_tensor(dn1[1:])

    (last_block,) = plain_call(
        input_grad_kernel,
        "input_grad",
        [array((block, model_width + EXTRA), BF16)],
        [],
        10 * block * model_width,
        meta,
        hidden_in,
        gain_rows,
        grad_resid,
        gains,
        *dn1,
    )
    layer_out, grad_input, grad_first_out, grad_second_out = plain_call(
        functools.partial(place_last_kernel, tensor_n),
        "place_last",
        [
            array((tokens_here, model_width), BF16),
            array((tokens_here, model_width), F32),
            array((1, rows), F32),
            array((1, rows), F32),
        ],
        [],
        tokens_here * model_width,
        meta,
        layer_block,
        *dn1[1:],
        *gather_tensor(last_block),
    )
    return (
        layer_out,
        grad_input,
        grad_first_out[0],
        grad_query,
        grad_key,
        grad_value,
        grad_outproj,
        grad_second_out[0],
        grad_router.T,
        grad_gate,
        grad_upproj,
        grad_down,
    )


def solution(mesh):
    tokens = P(("dp", "expert"), None)
    columns = P(None, "tensor")
    experts = P("expert", None, "tensor")
    rows = P(("dp", "expert"))
    both = P(("dp", "expert"), "tensor")
    expert_grads = P("expert", "dp", "tensor")
    return jax.shard_map(
        on_device,
        mesh=mesh,
        in_specs=(tokens, tokens, tokens, P())
        + (columns,) * 4
        + (P(), P())
        + (experts,) * 3
        + (tokens,),
        out_specs=(tokens, tokens, rows)
        + (both,) * 4
        + (rows, tokens)
        + (expert_grads,) * 3,
        check_vma=False,
    )
```

```python
import functools
import math

import jax
import jax.numpy as jnp
import numpy as np
from jax import lax
from jax.experimental import pallas as pl
from jax.experimental.pallas import tpu as pltpu
from jax.sharding import PartitionSpec as P

HD = 64
EPSILON = 1e-06
F32 = jnp.float32
BF16 = jnp.bfloat16
EXTRA = 128


def dot(left, right, dims):
    return lax.dot_general(left, right, (dims, ((), ())), preferred_element_type=F32)


def rope_tables(rows):
    inverse = np.exp(np.arange(HD // 2).astype(np.float32) * np.float32(-2.0 * math.log(1e4) / HD))
    angles = np.arange(rows, dtype=np.float32)[:, None] * inverse.astype(np.float32)[None, :]
    cosine, sine = np.cos(angles), np.sin(angles)
    return (
        jnp.asarray(np.concatenate([cosine] * 4, 1), F32),
        jnp.asarray(np.concatenate([-sine, sine] * 2, 1), F32),
    )


def other_halves(values):
    width = values.shape[1]
    lane = lax.broadcasted_iota(jnp.int32, values.shape, 1)
    return jnp.where(
        lane % HD < HD // 2,
        pltpu.roll(values, width - HD // 2, 1),
        pltpu.roll(values, HD // 2, 1),
    )


def widened(table, width):
    copies = width // table.shape[1]
    return table if copies == 1 else jnp.concatenate([table] * copies, 1)


def rotate(values, cosine, sine):
    width = values.shape[1]
    return values * widened(cosine, width) + other_halves(values) * widened(sine, width)


def rotate_back(values, cosine, sine):
    width = values.shape[1]
    return values * widened(cosine, width) - other_halves(values) * widened(sine, width)


def swap(x, axis, k):
    n = lax.axis_size(axis)
    return lax.ppermute(x, axis, [(i, i ^ k) for i in range(n)])


def swap_plane(x, k_dp, k_expert):
    n = lax.axis_size("expert")
    total = n * lax.axis_size("dp")
    return lax.ppermute(x, ("dp", "expert"), [(i, i ^ (k_dp * n + k_expert)) for i in range(total)])


def bits_of(n):
    k, out = n // 2, []
    while k >= 1:
        out.append(k)
        k //= 2
    return out


def gather_sets(x, near=None):
    bits = bits_of(lax.axis_size("expert"))
    sets = []
    for k_dp in range(lax.axis_size("dp")):
        if len(bits) == 2 and k_dp:
            parts = [swap(x, "dp", k_dp), swap_plane(x, k_dp, bits[0])]
            sets.append(parts + [swap(p, "expert", bits[1]) for p in parts])
            continue
        rows = swap(x, "dp", k_dp) if k_dp else x if near is None else near
        for k in bits[:-2]:
            rows = jnp.concatenate([rows, swap(rows, "expert", k)], 0)
        parts = [rows]
        for k in bits[-2:]:
            parts = parts + [swap(p, "expert", k) for p in parts]
        sets.append(parts)
    return sets


def swap_tensor(blocks):
    n = lax.axis_size("tensor")
    return [swap(blocks[k - 1], "tensor", k) for k in range(1, n)]


def gather_tensor(x):
    return [x] + swap_tensor([x] * (lax.axis_size("tensor") - 1))


def rows_at(index, rows):
    return pl.ds(pl.multiple_of(index * rows, rows), rows)


def plain_call(kernel, name, out_shape, scratch, flops, *arrays, after=(), hbm=(), vmem=16):
    def whole(a, far=False):
        if far:
            return pl.BlockSpec(memory_space=pltpu.HBM)
        if a.dtype == jnp.int32 and a.size <= 64:
            return pl.BlockSpec(memory_space=pltpu.SMEM)
        return pl.BlockSpec(a.shape, lambda i: (0,) * a.ndim)

    size = sum(a.size * a.dtype.itemsize for a in list(arrays) + list(out_shape))
    count, extra = len(arrays), len(after)

    def body(*refs):
        kernel(*refs[:count], *refs[count + extra :])

    arrays = list(arrays) + list(after)
    return pl.pallas_call(
        body,
        grid=(1,),
        in_specs=[whole(a, i in hbm) for i, a in enumerate(arrays[:count])] + [pl.BlockSpec(memory_space=pl.ANY)] * extra,
        out_specs=[whole(a) for a in out_shape],
        out_shape=out_shape,
        scratch_shapes=scratch,
        compiler_params=pltpu.CompilerParams(vmem_limit_bytes=vmem * 2**20),
        cost_estimate=pl.CostEstimate(flops=flops, bytes_accessed=size, transcendentals=0),
        name=name,
    )(*arrays)


def array(shape, dtype):
    return jax.ShapeDtypeStruct(shape, dtype)


def spread_blocks(me, value_ref, own_ref, sent_refs):
    rows = own_ref.shape[0]
    own_ref[...] = value_ref[rows_at(me, rows), :]
    for k, ref in enumerate(sent_refs, 1):
        ref[...] = value_ref[rows_at(me ^ k, rows), :].astype(ref.dtype)


def block_shapes(block, width, n):
    return [array((block, width), F32)] + [array((block, width), BF16)] * (n - 1)


def unit_rows(values):
    return lax.rsqrt(jnp.mean(values * values, -1, keepdims=True) + EPSILON)


def gain_row(ref):
    values = ref[...].astype(F32)
    return jnp.concatenate([values[i : i + 1, :] for i in range(values.shape[0])], 1)


def attend_kernel(heads, group, *refs):
    (meta, lengths, gain, cosine, sine) = refs[:5]
    far_refs, refs = refs[5:10], refs[10:]
    n1_ref, qkv_ref, prob_ref, att_ref, cos_ref, sin_ref = refs[:6]
    own_ref, *sent_refs = refs[6:-7]
    part_scr, hidden, query_w, key_w, value_w, output_w, sems = refs[-7:]
    near_refs = [hidden, query_w, key_w, value_w, output_w]
    copies = [
        pltpu.make_async_copy(far, near, sems.at[i])
        for i, (far, near) in enumerate(zip(far_refs, near_refs))
    ]
    for copy in copies:
        copy.start()
    copies[0].wait()
    x = hidden[...].astype(F32)
    n1 = (x * unit_rows(x) * gain_row(gain)).astype(BF16)
    n1_ref[...] = n1
    tokens = x.shape[0]
    rows = lax.broadcasted_iota(jnp.int32, (tokens, tokens), 0)
    columns = lax.broadcasted_iota(jnp.int32, (tokens, tokens), 1)
    table_rows = lax.broadcasted_iota(jnp.int32, cosine.shape, 0)
    cos, sin = cosine[...], sine[...]
    row_segment, column_segment = jnp.zeros_like(rows), jnp.zeros_like(rows)
    end = 0
    for i in range(lengths.shape[1] - 1):
        end = end + lengths[0, i]
        row_segment += (rows >= end).astype(jnp.int32)
        column_segment += (columns >= end).astype(jnp.int32)
        cos = jnp.where(table_rows >= end, pltpu.roll(cosine[...], end, 0), cos)
        sin = jnp.where(table_rows >= end, pltpu.roll(sine[...], end, 0), sin)
    cos_ref[...] = cos
    sin_ref[...] = sin
    allowed = (row_segment == column_segment) & (columns <= rows)
    q_width, kv_width = query_w.shape[1], key_w.shape[1]
    keys_at, values_at = q_width, q_width + kv_width
    for copy in copies[1:4]:
        copy.wait()
    qkv_ref[:, :q_width] = rotate(dot(n1, query_w[...], ((1,), (0,))), cos, sin).astype(BF16)
    qkv_ref[:, keys_at:values_at] = rotate(dot(n1, key_w[...], ((1,), (0,))), cos, sin).astype(BF16)
    qkv_ref[:, values_at:] = dot(n1, value_w[...], ((1,), (0,))).astype(BF16)
    for h in range(heads):
        g = h // group
        scores = dot(
            qkv_ref[:, h * HD : (h + 1) * HD],
            qkv_ref[:, keys_at + g * HD : keys_at + (g + 1) * HD],
            ((1,), (1,)),
        )
        masked = jnp.where(allowed, scores * HD ** (-0.5), -1e30)
        exponent = jnp.exp(masked - jnp.max(masked, -1, keepdims=True))
        prob = exponent / jnp.sum(exponent, -1, keepdims=True)
        prob_ref[h] = prob
        head_out = dot(
            prob.astype(BF16), qkv_ref[:, values_at + g * HD : values_at + (g + 1) * HD], ((1,), (0,))
        )
        att_ref[:, h * HD : (h + 1) * HD] = head_out.astype(BF16)
    for copy in copies[4:]:
        copy.wait()
    part_scr[...] = dot(att_ref[...], output_w[...], ((1,), (1,)))
    spread_blocks(meta[0], part_scr, own_ref, sent_refs)
    own_ref[...] += hidden[rows_at(meta[0], own_ref.shape[0]), :].astype(F32)


def fill_routes(routes, out_ref):
    width = out_ref.shape[1] - EXTRA
    named = routes[...].astype(F32).T
    lane = lax.broadcasted_iota(jnp.int32, (out_ref.shape[0], EXTRA), 1).astype(F32)
    total = jnp.zeros(lane.shape, F32)
    for j in range(named.shape[1]):
        total += (named[:, j : j + 1] == lane).astype(F32)
    out_ref[:, width:] = total.astype(BF16)


def second_norm_kernel(gain, grad, *refs):
    parts, (residual_ref, n2_ref, grad_ref) = refs[:-3], refs[-3:]
    grad_ref[...] = grad[...]
    residual = parts[0][...]
    for part in parts[1:]:
        residual = residual + part[...].astype(F32)
    residual_ref[...] = residual
    n2_ref[...] = (residual * unit_rows(residual) * gain_row(gain)).astype(BF16)


def place_second_kernel(meta, routes, *refs):
    blocks, out_ref = refs[:-1], refs[-1]
    rows, width = blocks[0].shape
    for k, ref in enumerate(blocks):
        out_ref[rows_at(meta[0] ^ k, rows), :width] = ref[...]
    fill_routes(routes, out_ref)


def halves_kernel(meta, near, got, last, *refs):
    own_ref, *sent_refs = refs[:-1]
    total_scr = refs[-1]
    rows = last.shape[0]
    total_scr[...] = (
        near[:rows, :].astype(F32) + got[:rows, :].astype(F32) + last[...].astype(F32)
    )
    spread_blocks(meta[0], total_scr, own_ref, sent_refs)


def residual_grad_kernel(experts, tensor_n, meta, residual_ref, n2_ref, dy_ref, router, gain, *refs):
    mixed_near, mixed_got, mixed_last = refs[:3]
    parts, refs = refs[3 : 3 + tensor_n], refs[3 + tensor_n :]
    dh_ref, gain_row_ref, message_ref, mixed_ref, *sent_refs = refs[:-1]
    mixed_scr = refs[-1]
    tokens = dy_ref.shape[0]
    mixed_scr[...] = (
        mixed_near[:tokens, :].astype(F32)
        + mixed_got[:tokens, :].astype(F32)
        + mixed_last[...].astype(F32)
    )
    block, width = residual_ref.shape
    mine = rows_at(meta[0], block)
    arrival = parts[0][...]
    for part in parts[1:]:
        arrival = arrival + part[...].astype(F32)
    logits = dot(n2_ref[mine, :width], router[...], ((1,), (1,)))
    routed = n2_ref[mine, width : width + experts].astype(F32) > 0.5
    logits = jnp.where(routed, logits, -1e30)
    gates = jnp.exp(logits - jnp.max(logits, -1, keepdims=True))
    gates = gates / jnp.sum(gates, -1, keepdims=True)
    extra = arrival[:, width:]
    dg = extra[:, :experts] + pltpu.roll(extra, EXTRA - experts, 1)[:, :experts]
    dlog = gates * (dg - jnp.sum(gates * dg, -1, keepdims=True))
    high = dlog.astype(BF16)
    low = (dlog - high.astype(F32)).astype(BF16)
    dn2 = (
        arrival[:, :width]
        + dot(high, router[...], ((1,), (0,)))
        + dot(low, router[...], ((1,), (0,)))
    )
    residual = residual_ref[...]
    scale = unit_rows(residual)
    hat = residual * scale
    gain_row_ref[...] = jnp.zeros_like(gain_row_ref)
    gain_row_ref[0:1, :] = jnp.sum(dn2 * hat, 0, keepdims=True)
    gained = dn2 * gain_row(gain)
    dh = dy_ref[mine, :].astype(F32) + scale * (
        gained - hat * jnp.mean(gained * hat, -1, keepdims=True)
    )
    dh_ref[...] = dh
    message_ref[:, :width] = dh.astype(BF16)
    message_ref[:, width:] = jnp.zeros((block, EXTRA), BF16)
    message_ref[:, width : width + experts] = high
    message_ref[:, width + experts : width + 2 * experts] = low
    mixed_ref[...] = mixed_scr[mine, :]
    for k, ref in enumerate(sent_refs, 1):
        ref[:, : width + EXTRA] = message_ref[...]
        ref[:, width + EXTRA :] = mixed_scr[rows_at(meta[0] ^ k, block), :].astype(BF16)


def attend_grad_kernel(heads, group, experts, expert_n, dp_n, tensor_n, *refs):
    (meta, hidden, gain_row, n1_ref, n2_ref, qkv_ref, prob_ref, att_ref, cos_ref, sin_ref) = refs[:10]
    query_w, key_w, value_w, output_w = refs[10:14]
    messages = refs[14 : 14 + tensor_n]
    mixed_own, residual_ref = refs[14 + tensor_n : 16 + tensor_n]
    near_ref, far_ref, layer_ref, own_ref, *sent_refs = refs[16 + tensor_n : -6]
    dh_scr, dqkv_scr, raw_scr, dn1_scr, left_scr, side_scr = refs[-6:]
    block = messages[0].shape[0]
    width = hidden.shape[1]
    for k, ref in enumerate(messages):
        dh_scr[rows_at(meta[0] ^ k, block), :] = ref[:, : width + EXTRA]
    cos, sin = cos_ref[...], sin_ref[...]
    q_width, kv_width = query_w.shape[1], key_w.shape[1]
    keys_at, values_at = q_width, q_width + kv_width
    dob = dh_scr[:, :width]
    da = dot(dob, output_w[...], ((1,), (0,))).astype(BF16)
    scale = HD ** (-0.5)
    for g in range(heads // group):
        key = qkv_ref[:, keys_at + g * HD : keys_at + (g + 1) * HD]
        value = qkv_ref[:, values_at + g * HD : values_at + (g + 1) * HD]
        dk = dv = 0.0
        for h in range(g * group, (g + 1) * group):
            da_h = da[:, h * HD : (h + 1) * HD]
            prob = prob_ref[h]
            dprob = dot(da_h, value, ((1,), (1,)))
            ds = prob * (dprob - jnp.sum(prob * dprob, -1, keepdims=True))
            raw_scr[:, h * HD : (h + 1) * HD] = dot(ds.astype(BF16), key, ((1,), (0,))) * scale
            dk = dk + dot(ds.T.astype(BF16), qkv_ref[:, h * HD : (h + 1) * HD], ((1,), (0,)))
            dv = dv + dot(prob.T.astype(BF16), da_h, ((1,), (0,)))
        raw_scr[:, keys_at + g * HD : keys_at + (g + 1) * HD] = dk * scale
        dqkv_scr[:, values_at + g * HD : values_at + (g + 1) * HD] = dv.astype(BF16)
    dqkv_scr[:, :q_width] = rotate_back(raw_scr[:, :q_width], cos, sin).astype(BF16)
    dqkv_scr[:, keys_at:values_at] = rotate_back(raw_scr[:, keys_at:values_at], cos, sin).astype(BF16)
    dn1 = (
        dot(dqkv_scr[:, :q_width], query_w[...], ((1,), (1,)))
        + dot(dqkv_scr[:, keys_at:values_at], key_w[...], ((1,), (1,)))
        + dot(dqkv_scr[:, values_at:], value_w[...], ((1,), (1,)))
    )
    dn1_scr[...] = dn1
    layer = residual_ref[...] + mixed_own[...]
    for ref in messages[1:]:
        layer = layer + ref[:, width + EXTRA :].astype(F32)
    layer_ref[...] = layer.astype(BF16)
    own_ref[...] = dn1_scr[rows_at(meta[0], block), :]
    for k, ref in enumerate(sent_refs, 1):
        ref[:, :width] = dn1_scr[rows_at(meta[0] ^ k, block), :].astype(BF16)
        ref[:, width:] = layer.astype(BF16)
    x = hidden[...].astype(F32)
    first_row = jnp.sum(dn1 * (x * unit_rows(x)), 0, keepdims=True)
    dlog_t = dh_scr[:, width:].astype(F32).T.astype(BF16)
    router_t = dot(dlog_t, n2_ref[:, :width], ((1,), (0,)))
    router_t = router_t[:experts] + router_t[experts : 2 * experts]
    side = jnp.concatenate(
        [router_t, gain_row[0:1, :], first_row, jnp.zeros((EXTRA - experts - 2, width), F32)], 0
    )
    side_scr[...] = side.T.astype(BF16)
    left_scr[:width, :] = n1_ref[...].T
    left_scr[width:, :] = dob.T
    places = expert_n * dp_n
    rows = width // places
    expert_bits = list(reversed(bits_of(expert_n)))
    qkv_width = values_at + kv_width
    for at in range(places):
        bits = [(at // (places >> (i + 1))) % 2 for i in range(len(expert_bits))]
        e_rel = sum(b * k for b, k in zip(bits, expert_bits))
        index = (meta[2] ^ (at % dp_n)) * expert_n + (meta[1] ^ e_rel)
        out = near_ref if at < places // 2 else far_ref
        to = slice((at % (places // 2)) * rows, (at % (places // 2) + 1) * rows)
        source = rows_at(index, rows)
        out[to, :qkv_width] = dot(left_scr[source, :], dqkv_scr[...], ((1,), (0,))).astype(BF16)
        out[to, qkv_width : qkv_width + EXTRA] = side_scr[source, :]
        below = left_scr[rows_at(index + places, rows), :]
        out[to, qkv_width + EXTRA :] = dot(below, att_ref[...], ((1,), (0,))).astype(BF16)


def input_grad_kernel(meta, hidden, gain, dh_ref, gains_ref, *refs):
    parts, out_ref = refs[:-1], refs[-1]
    block, width = dh_ref.shape
    dn1 = parts[0][...]
    for part in parts[1:]:
        dn1 = dn1 + part[:, :width].astype(F32)
    x = hidden[rows_at(meta[0], block), :].astype(F32)
    scale = unit_rows(x)
    hat = x * scale
    gained = dn1 * gain_row(gain)
    grad = dh_ref[...] + scale * (gained - hat * jnp.mean(gained * hat, -1, keepdims=True))
    out_ref[:, :width] = grad.astype(BF16)
    rows, columns = gains_ref.shape
    gains = gains_ref[...]
    high = gains.astype(BF16).astype(F32)
    out_ref[:, width:] = jnp.zeros((block, EXTRA), BF16)
    out_ref[: 2 * rows, width : width + columns] = jnp.concatenate(
        [high, gains - high], 0
    ).astype(BF16)


def place_last_kernel(tensor_n, meta, layer_own, *refs):
    layers, blocks = refs[: tensor_n - 1], refs[tensor_n - 1 : -4]
    layer_ref, grad_ref, first_ref, second_ref = refs[-4:]
    rows, width = layer_own.shape
    layer_ref[rows_at(meta[0], rows), :] = layer_own[...]
    for k, ref in enumerate(layers, 1):
        layer_ref[rows_at(meta[0] ^ k, rows), :] = ref[:, width:]
    gains = 0.0
    for k, ref in enumerate(blocks):
        grad_ref[rows_at(meta[0] ^ k, rows), :] = ref[:, :width].astype(F32)
        gains = gains + ref[:16, width:].astype(F32)
    gains = gains[:8] + gains[8:]
    columns = first_ref.shape[1]
    second_ref[...] = gains[0:1, :columns]
    first_ref[...] = gains[1:2, :columns]


def half_kernel(near, got, out_ref):
    half = out_ref.shape[0]
    out_ref[...] = (near[half:, :].astype(F32) + got[half:, :].astype(F32)).astype(BF16)


def add_kernel(near, got, own_ref, *sent_refs):
    rows = own_ref.shape[0]
    for k, ref in enumerate([own_ref] + list(sent_refs)):
        at = slice(k * rows, (k + 1) * rows)
        ref[...] = (near[at, :].astype(F32) + got[at, :].astype(F32)).astype(ref.dtype)


def last_kernel(experts, q_width, kv_width, *refs):
    parts, outs = refs[:-6], refs[-6:]
    total = parts[0][...]
    for part in parts[1:]:
        total = total + part[...].astype(F32)
    at = 0
    for ref, width in zip(outs[:3], (q_width, kv_width, kv_width)):
        ref[...] = total[:, at : at + width]
        at += width
    side = total[:, at : at + EXTRA]
    outs[3][...] = total[:, at + EXTRA :]
    side = side.T
    outs[4][...] = side[:experts]
    outs[5][...] = side[experts : experts + 8]


def pair_of(local_experts):
    return 2 if local_experts % 2 == 0 else 1


def kernel_params(tokens, vmem=28):
    return pltpu.CompilerParams(vmem_limit_bytes=(vmem if tokens <= 512 else 60) * 2**20)


def side_by_side(ref, first, count):
    parts = [ref[first + i] for i in range(count)]
    return parts[0] if count == 1 else jnp.concatenate(parts, 1)


def split_rows(chunk, chunks, value, near_ref, far_ref):
    if chunks == 1:
        half = value.shape[0] // 2
        near_ref[...] = value[:half]
        far_ref[...] = value[half:]
        return
    rows = value.shape[0]

    @pl.when(chunk < chunks // 2)
    def _():
        near_ref[pl.ds(pl.multiple_of(chunk * rows, rows), rows), :] = value

    @pl.when(chunk >= chunks // 2)
    def _():
        at = (chunk - chunks // 2) * rows
        far_ref[pl.ds(pl.multiple_of(at, rows), rows), :] = value


def expert_kernel(own, steps, pair, experts, parts, extra, *refs):
    meta_ref, refs = refs[0], refs[1:]
    x_parts, dy_parts, refs = refs[:parts], refs[parts : 2 * parts], refs[2 * parts :]
    gate_ref, up_ref, down_ref, router_ref = refs[:4]
    refs = refs[extra:]
    both_ref, gated_ref = refs[4:6]
    if own:
        dg_ref, dg_scr = refs[6], refs[-1]
        refs = refs[7:-1]
    else:
        refs = refs[6:]
    gates_scr, x_ref, dy_ref = refs
    step = pl.program_id(1)
    width = dy_ref.shape[1]
    lanes = gates_scr.shape[1]

    @pl.when(step == 0)
    def _():
        part_rows = x_parts[0].shape[0]
        for n in range(parts):
            x_ref[n * part_rows : (n + 1) * part_rows, :] = x_parts[n][...]
            dy_ref[n * part_rows : (n + 1) * part_rows, :] = dy_parts[n][...]
        logits = dot(x_ref[:, :width], router_ref[...], ((1,), (1,)))
        routed = x_ref[:, width : width + experts].astype(F32) > 0.5
        logits = jnp.where(routed, logits, -1e30)
        weights = jnp.exp(logits - jnp.max(logits, -1, keepdims=True))
        gates_scr[...] = jnp.zeros_like(gates_scr)
        gates_scr[:, :experts] = weights / jnp.sum(weights, -1, keepdims=True)
        if own:
            dg_scr[...] = jnp.zeros_like(dg_scr)

    first = meta_ref[1] * (pair * steps) + step * pair
    gates = pltpu.roll(gates_scr[...], lax.rem(lanes - first, lanes), 1)
    raw_all = dot(dy_ref[...], side_by_side(down_ref, 0, pair), ((1,), (0,)))
    units = gate_ref.shape[2]
    column = lax.broadcasted_iota(jnp.int32, gates.shape, 1)
    weight = jnp.concatenate([r[i] for i in range(pair) for r in (gate_ref, up_ref)], 1)
    both_all = dot(x_ref[:, :width], weight, ((1,), (0,)))
    for i in range(pair):
        gate_proj = both_all[:, 2 * i * units : (2 * i + 1) * units]
        up_proj = both_all[:, (2 * i + 1) * units : (2 * i + 2) * units]
        raw = raw_all[:, i * units : (i + 1) * units]
        mine = gates[:, i : i + 1]
        sigmoid_gate = 0.5 * jnp.tanh(0.5 * gate_proj) + 0.5
        activated = gate_proj * sigmoid_gate
        hidden = activated * up_proj
        grad_hidden = raw * mine
        grad_gate = grad_hidden * up_proj * (sigmoid_gate + activated * (1.0 - sigmoid_gate))
        at = 2 * i * units
        both_ref[:, at : at + units] = grad_gate.astype(BF16)
        both_ref[:, at + units : at + 2 * units] = (grad_hidden * activated).astype(BF16)
        gated_ref[:, i * units : (i + 1) * units] = (hidden * mine).astype(BF16)
        if own:
            dg = jnp.sum(raw * hidden, 1, keepdims=True)
            dg_scr[...] += jnp.where(column == first + i, dg, 0.0)
    if own:

        @pl.when(step == steps - 1)
        def _():
            dg = dg_scr[...]
            high = dg.astype(BF16).astype(F32)
            low = pltpu.roll(dg - high, experts, 1)
            dg_ref[...] = (high + low).astype(BF16)


def expert_call(own, meta, xs, dys, gate_weight, up_weight, down_weight, router_weight, after=()):
    part_rows, width = dys[0].shape
    parts = len(xs)
    tokens = part_rows * parts
    if tokens > 512:
        xs, dys, parts = [jnp.concatenate(xs, 0)], [jnp.concatenate(dys, 0)], 1
        part_rows = tokens
    x_width = xs[0].shape[1]
    local, _, units = gate_weight.shape
    experts = router_weight.shape[0]
    pair = pair_of(local)
    rows = min(tokens, 512)
    chunks, steps = tokens // rows, local // pair
    grid_spec = dict(
        grid=(chunks, steps),
        in_specs=[
            pl.BlockSpec(memory_space=pltpu.SMEM),
        ]
        + [pl.BlockSpec((rows // parts, x_width), lambda c, s: (c, 0))] * parts
        + [pl.BlockSpec((rows // parts, width), lambda c, s: (c, 0))] * parts
        + [pl.BlockSpec((pair, width, units), lambda c, s: (s, 0, 0))] * 3
        + [pl.BlockSpec(router_weight.shape, lambda c, s: (0, 0))]
        + [pl.BlockSpec(memory_space=pl.ANY)] * len(after),
        out_specs=[
            pl.BlockSpec((rows, pair * 2 * units), lambda c, s: (c, s)),
            pl.BlockSpec((rows, pair * units), lambda c, s: (c, s)),
        ],
        scratch_shapes=[
            pltpu.VMEM((rows, 128), F32),
            pltpu.VMEM((rows, x_width), BF16),
            pltpu.VMEM((rows, width), BF16),
        ],
    )
    out_shape = [
        jax.ShapeDtypeStruct((tokens, local * 2 * units), BF16),
        jax.ShapeDtypeStruct((tokens, local * units), BF16),
    ]
    if own:
        grid_spec["out_specs"] += [pl.BlockSpec((rows, EXTRA), lambda c, s: (c, 0))]
        out_shape += [jax.ShapeDtypeStruct((tokens, EXTRA), BF16)]
        grid_spec["scratch_shapes"] += [pltpu.VMEM((rows, 128), F32)]
    products = 3
    return pl.pallas_call(
        functools.partial(expert_kernel, own, steps, pair, experts, parts, len(after)),
        out_shape=out_shape,
        compiler_params=kernel_params(tokens),
        cost_estimate=pl.CostEstimate(
            flops=2 * products * tokens * width * local * units,
            bytes_accessed=2 * (3 * local * width * units + 3 * tokens * width),
            transcendentals=tokens * local * units,
        ),
        name="experts_own" if own else "experts_far",
        **grid_spec,
    )(meta, *xs, *dys, gate_weight, up_weight, down_weight, router_weight, *after)


def arrival_kernel(chunks, steps, pair, both_ref, dg_ref, gate_ref, up_ref, *refs):
    near_ref, far_ref, total_scr = refs[-3:]
    chunk, step = pl.program_id(0), pl.program_id(1)

    @pl.when(step == 0)
    def _():
        total_scr[...] = jnp.zeros_like(total_scr)

    weight = jnp.concatenate([r[i] for i in range(pair) for r in (gate_ref, up_ref)], 1)
    total_scr[...] += dot(both_ref[...], weight, ((1,), (1,)))

    @pl.when(step == steps - 1)
    def _():
        message = jnp.concatenate([total_scr[...].astype(BF16), dg_ref[...]], 1)
        split_rows(chunk, chunks, message, near_ref, far_ref)


def arrival_call(both, dg, gate_weight, up_weight, after=()):
    tokens = both.shape[0]
    local, width, units = gate_weight.shape
    pair = pair_of(local)
    rows = min(tokens, 512)
    chunks, steps = tokens // rows, local // pair
    half = (tokens // 2, width + EXTRA)
    return pl.pallas_call(
        functools.partial(arrival_kernel, chunks, steps, pair),
        grid=(chunks, steps),
        in_specs=[
            pl.BlockSpec((rows, pair * 2 * units), lambda c, s: (c, s)),
            pl.BlockSpec((rows, EXTRA), lambda c, s: (c, 0)),
        ]
        + [pl.BlockSpec((pair, width, units), lambda c, s: (s, 0, 0))] * 2
        + [pl.BlockSpec(memory_space=pl.ANY)] * len(after),
        out_specs=[pl.BlockSpec(half, lambda c, s: (0, 0))] * 2,
        out_shape=[jax.ShapeDtypeStruct(half, BF16)] * 2,
        scratch_shapes=[pltpu.VMEM((rows, width), F32)],
        compiler_params=kernel_params(tokens),
        cost_estimate=pl.CostEstimate(
            flops=4 * tokens * width * local * units,
            bytes_accessed=4 * (local * width * units + 2 * tokens * width),
            transcendentals=0,
        ),
        name="experts_arrival",
    )(both, dg, gate_weight, up_weight, *after)


def mixed_kernel(chunks, steps, pair, gated_ref, down_ref, *refs):
    near_ref, far_ref, total_scr = refs[-3:]
    chunk, step = pl.program_id(0), pl.program_id(1)

    @pl.when(step == 0)
    def _():
        total_scr[...] = jnp.zeros_like(total_scr)

    total_scr[...] += dot(gated_ref[...], side_by_side(down_ref, 0, pair), ((1,), (1,)))

    @pl.when(step == steps - 1)
    def _():
        split_rows(chunk, chunks, total_scr[...].astype(BF16), near_ref, far_ref)


def mixed_call(gated, down_weight, after=()):
    tokens = gated.shape[0]
    local, width, units = down_weight.shape
    pair = pair_of(local)
    rows = min(tokens, 512)
    chunks, steps = tokens // rows, local // pair
    half = (tokens // 2, width)
    return pl.pallas_call(
        functools.partial(mixed_kernel, chunks, steps, pair),
        grid=(chunks, steps),
        in_specs=[
            pl.BlockSpec((rows, pair * units), lambda c, s: (c, s)),
            pl.BlockSpec((pair, width, units), lambda c, s: (s, 0, 0)),
        ]
        + [pl.BlockSpec(memory_space=pl.ANY)] * len(after),
        out_specs=[pl.BlockSpec(half, lambda c, s: (0, 0))] * 2,
        out_shape=[jax.ShapeDtypeStruct(half, BF16)] * 2,
        scratch_shapes=[pltpu.VMEM((rows, width), F32)],
        compiler_params=kernel_params(tokens),
        cost_estimate=pl.CostEstimate(
            flops=2 * tokens * width * local * units,
            bytes_accessed=2 * (local * width * units + 2 * tokens * width),
            transcendentals=0,
        ),
        name="experts_mixed",
    )(gated, down_weight, *after)


def weight_grad_kernel(sets, parts, outs, pair, units, place_ref, *refs):
    lefts, rights = refs[: sets * parts], refs[sets * parts : sets * parts + sets]
    grad_refs, token_ref = refs[-4 - outs : -4], refs[-4]
    left_scr, out_scr, sems = refs[-3:]
    token_ref[...] = jnp.zeros_like(token_ref)
    step, steps = pl.program_id(0), pl.num_programs(0)
    slot = lax.rem(step, 2)

    def copies(at, which):
        return [
            pltpu.make_async_copy(
                out_scr.at[which, j], grad_refs[j].at[pl.ds(at * pair, pair)], sems.at[which, j]
            )
            for j in range(outs)
        ]

    @pl.when(pl.program_id(0) == 0)
    def _():
        for n in range(sets * parts):
            rows = lefts[n].shape[0]
            left_scr[:, n * rows : (n + 1) * rows] = lefts[n][...].T

    rows = rights[0].shape[0]
    total = None
    for n in range(sets):
        part = dot(left_scr[:, n * rows : (n + 1) * rows], rights[n][...], ((1,), (0,)))
        total = part if total is None else total + part

    @pl.when(step >= 2)
    def _():
        for copy in copies(step - 2, slot):
            copy.wait()

    for i in range(pair):
        for j in range(outs):
            at = (i * outs + j) * units
            out_scr[slot, j, i] = total[:, at : at + units]
    for copy in copies(step, slot):
        copy.start()

    @pl.when(step == steps - 1)
    def _():
        for copy in copies(step, slot):
            copy.wait()

    @pl.when((step == steps - 1) & (step >= 1))
    def _():
        for copy in copies(step - 1, 1 - slot):
            copy.wait()


def weight_grad_call(meta, lefts, rights, local, units, after=()):
    sets, parts = len(lefts), len(lefts[0])
    outs = rights[0].shape[1] // (local * units)
    part_rows = lefts[0][0].shape[0]
    width = lefts[0][0].shape[1] // 128 // sets * 128
    tokens = part_rows * parts
    lefts = sum(lefts, [])
    pair = pair_of(local)
    columns = pl.BlockSpec(
        (part_rows, width), lambda s, meta: (0, meta[2]), pipeline_mode=pl.Buffered(1)
    )
    return pl.pallas_call(
        functools.partial(weight_grad_kernel, sets, parts, outs, pair, units),
        grid_spec=pltpu.PrefetchScalarGridSpec(
            num_scalar_prefetch=1,
            grid=(local // pair,),
            in_specs=[columns] * (sets * parts)
            + [pl.BlockSpec((tokens, pair * outs * units), lambda s, meta: (0, s))] * sets
            + [pl.BlockSpec(memory_space=pl.ANY)] * len(after),
            out_specs=[pl.BlockSpec(memory_space=pltpu.HBM)] * outs
            + [pl.BlockSpec((8, 128), lambda s, meta: (0, 0))],
            scratch_shapes=[
                pltpu.VMEM((width, sets * tokens), BF16),
                pltpu.VMEM((2, outs, pair, width, units), F32),
                pltpu.SemaphoreType.DMA((2, outs)),
            ],
        ),
        out_shape=[array((local, width, units), F32)] * outs + [array((8, 128), F32)],
        compiler_params=kernel_params(tokens),
        cost_estimate=pl.CostEstimate(
            flops=2 * sets * tokens * width * outs * local * units,
            bytes_accessed=4 * outs * local * width * units + 4 * sets * tokens * width,
            transcendentals=0,
        ),
        name="experts_weight_grads",
    )(meta, *lefts, *rights, *after)


def reduce_first(near, far, after=()):
    bits = list(reversed(bits_of(lax.axis_size("expert"))))
    for k in bits[:-2]:
        got = swap(far, "expert", k)
        total = (near.astype(F32) + got.astype(F32)).astype(BF16)
        near, far = jnp.split(total, 2, 0)
    got = swap(far, "expert", bits[-2])
    half = near.shape[0] // 2
    if after:
        (sent,) = plain_call(
            half_kernel,
            "half",
            [array((half, near.shape[1]), BF16)],
            [],
            near.size,
            near,
            got,
            after=after,
        )
    else:
        sent = (near[half:].astype(F32) + got[half:].astype(F32)).astype(BF16)
    return near, got, swap(sent, "expert", bits[-1])


def on_device(
    hidden_in,
    seq_lengths,
    expert_routes,
    first_gain,
    query_weight,
    key_weight,
    value_weight,
    output_weight,
    second_gain,
    router_weight,
    gate_weight,
    up_weight,
    down_weight,
    grad_layer_out,
):
    tokens_here, model_width = hidden_in.shape
    q_width, kv_width = query_weight.shape[1], key_weight.shape[1]
    heads, group = q_width // HD, q_width // kv_width
    expert_count = router_weight.shape[1]
    local_experts, _, units = gate_weight.shape
    tensor_n = lax.axis_size("tensor")
    expert_n = lax.axis_size("expert")
    dp_n = lax.axis_size("dp")
    block = tokens_here // tensor_n
    meta = jnp.stack([lax.axis_index(a) for a in ("tensor", "expert", "dp")]).astype(jnp.int32)
    first_tile, second_tile = first_gain.reshape(-1, 128), second_gain.reshape(-1, 128)

    cosine, sine = rope_tables(tokens_here)
    blocks = block_shapes(block, model_width, tensor_n)
    outs = plain_call(
        functools.partial(attend_kernel, heads, group),
        "attend",
        [
            array((tokens_here, model_width), BF16),
            array((tokens_here, q_width + 2 * kv_width), BF16),
            array((heads, tokens_here, tokens_here), F32),
            array((tokens_here, q_width), BF16),
            array(cosine.shape, F32),
            array(sine.shape, F32),
        ]
        + blocks,
        [
            pltpu.VMEM((tokens_here, model_width), F32),
            pltpu.VMEM(hidden_in.shape, BF16),
            pltpu.VMEM(query_weight.shape, BF16),
            pltpu.VMEM(key_weight.shape, BF16),
            pltpu.VMEM(value_weight.shape, BF16),
            pltpu.VMEM(output_weight.shape, BF16),
            pltpu.SemaphoreType.DMA((5,)),
        ],
        2 * tokens_here * model_width * 3 * q_width,
        meta,
        seq_lengths,
        first_tile,
        cosine,
        sine,
        hidden_in,
        query_weight,
        key_weight,
        value_weight,
        output_weight,
        hbm=range(5, 10),
        vmem=60,
    )
    n1, qkv, prob, att, cosine, sine, part, *sent = outs
    far_grads = [swap(grad_layer_out, "dp", k) for k in range(1, dp_n)]
    if expert_n == 4:
        far_grads += [swap_plane(grad_layer_out, k, 2) for k in range(1, dp_n)]
    residual, second_block, grad_near = plain_call(
        second_norm_kernel,
        "second_norm",
        [
            array((block, model_width), F32),
            array((block, model_width), BF16),
            array(grad_layer_out.shape, BF16),
        ],
        [],
        8 * block * model_width,
        second_tile,
        grad_layer_out,
        part,
        *swap_tensor(sent),
        after=far_grads,
    )
    grad_sets = gather_sets(grad_layer_out, grad_near)
    (second_group,) = plain_call(
        place_second_kernel,
        "place_second",
        [array((tokens_here, model_width + EXTRA), BF16)],
        [],
        tokens_here * model_width,
        meta,
        expert_routes.T,
        *gather_tensor(second_block),
        after=grad_sets[0][1:2],
    )
    second_sets = gather_sets(second_group)

    router_t = router_weight.T
    weights = (gate_weight, up_weight, down_weight, router_t)
    far_grads = [g for x in grad_sets[1:] for g in x[:2]]
    own = expert_call(True, meta, second_sets[0], grad_sets[0], *weights, after=far_grads)
    arrival = arrival_call(
        own[0], own[2], gate_weight, up_weight, after=[x for y in second_sets[1:] for x in y[:2]]
    )
    sides = [own] + [
        expert_call(False, meta, second_sets[i], grad_sets[i], *weights) for i in range(1, dp_n)
    ]
    mixed = mixed_call(own[1], down_weight, after=arrival[:1])
    arrival = plain_call(
        halves_kernel,
        "arrival_blocks",
        block_shapes(block, model_width + EXTRA, tensor_n),
        [pltpu.VMEM((tokens_here, model_width + EXTRA), F32)],
        2 * tokens_here * model_width,
        meta,
        *reduce_first(*arrival),
        after=[mixed[0]] + [x[1] for x in sides[1:]],
    )
    mixed = reduce_first(*mixed, after=arrival[:1])
    arrival = [arrival[0]] + swap_tensor(arrival[1:])
    grad_down, down_done = weight_grad_call(
        meta, grad_sets, [x[1] for x in sides], local_experts, units
    )
    grad_gate, grad_upproj, gate_done = weight_grad_call(
        meta, second_sets, [x[0] for x in sides], local_experts, units
    )

    grad_resid, gain_row, message, mixed_own, *sent = plain_call(
        functools.partial(residual_grad_kernel, expert_count, tensor_n),
        "residual_grad",
        [
            array((block, model_width), F32),
            array((8, model_width), F32),
            array((block, model_width + EXTRA), BF16),
            array((block, model_width), F32),
        ]
        + [array((block, 2 * model_width + EXTRA), BF16)] * (tensor_n - 1),
        [pltpu.VMEM((tokens_here, model_width), F32)],
        20 * block * model_width,
        meta,
        residual,
        second_group,
        grad_layer_out,
        router_t,
        second_tile,
        *mixed,
        *arrival,
        after=[down_done],
    )
    places = expert_n * dp_n
    rows = model_width // places
    last_width = 2 * q_width + 2 * kv_width + EXTRA
    near, far, layer_block, *dn1 = plain_call(
        functools.partial(
            attend_grad_kernel, heads, group, expert_count, expert_n, dp_n, tensor_n
        ),
        "attend_grad",
        [array((model_width // 2, last_width), BF16)] * 2
        + [array((block, model_width), BF16), array((block, model_width), F32)]
        + [array((block, 2 * model_width), BF16)] * (tensor_n - 1),
        [
            pltpu.VMEM((tokens_here, model_width + EXTRA), BF16),
            pltpu.VMEM((tokens_here, q_width + 2 * kv_width), BF16),
            pltpu.VMEM((tokens_here, q_width + kv_width), F32),
            pltpu.VMEM((tokens_here, model_width), F32),
            pltpu.VMEM((2 * model_width, tokens_here), BF16),
            pltpu.VMEM((model_width, EXTRA), BF16),
        ],
        2 * tokens_here * model_width * 6 * q_width,
        meta,
        hidden_in,
        gain_row,
        n1,
        second_group,
        qkv,
        prob,
        att,
        cosine,
        sine,
        query_weight,
        key_weight,
        value_weight,
        output_weight,
        message,
        *swap_tensor(sent),
        mixed_own,
        residual,
        after=[gate_done],
    )

    expert_bits = list(reversed(bits_of(expert_n)))
    for k in expert_bits[:-2]:
        total = near.astype(F32) + swap(far, "expert", k).astype(F32)
        near, far = jnp.split(total.astype(BF16), 2, 0)
    got = swap(far, "expert", expert_bits[-2])
    shapes = [array((rows, last_width), F32)] + [array((rows, last_width), BF16)] * (2 * dp_n - 1)
    own_rows, *sent = plain_call(
        add_kernel, "plane_add", shapes, [], model_width * last_width, near, got
    )
    ways = [(k % dp_n, (k // dp_n) * expert_bits[-1]) for k in range(1, 2 * dp_n)]
    got = [swap_plane(x, *way) for x, way in zip(sent, ways)]
    grad_query, grad_key, grad_value, grad_outproj, grad_router, gains = plain_call(
        functools.partial(last_kernel, expert_count, q_width, kv_width),
        "plane_last",
        [
            array((rows, q_width), F32),
            array((rows, kv_width), F32),
            array((rows, kv_width), F32),
            array((rows, q_width), F32),
            array((expert_count, rows), F32),
            array((8, rows), F32),
        ],
        [],
        4 * rows * last_width,
        own_rows,
        *got,
    )
    dn1 = [dn1[0]] + swap_tensor(dn1[1:])

    (last_block,) = plain_call(
        input_grad_kernel,
        "input_grad",
        [array((block, model_width + EXTRA), BF16)],
        [],
        10 * block * model_width,
        meta,
        hidden_in,
        first_tile,
        grad_resid,
        gains,
        *dn1,
    )
    layer_out, grad_input, grad_first_out, grad_second_out = plain_call(
        functools.partial(place_last_kernel, tensor_n),
        "place_last",
        [
            array((tokens_here, model_width), BF16),
            array((tokens_here, model_width), F32),
            array((1, rows), F32),
            array((1, rows), F32),
        ],
        [],
        tokens_here * model_width,
        meta,
        layer_block,
        *dn1[1:],
        *gather_tensor(last_block),
    )
    return (
        layer_out,
        grad_input,
        grad_first_out[0],
        grad_query,
        grad_key,
        grad_value,
        grad_outproj,
        grad_second_out[0],
        grad_router.T,
        grad_gate,
        grad_upproj,
        grad_down,
    )


def solution(mesh):
    tokens = P(("dp", "expert"), None)
    columns = P(None, "tensor")
    experts = P("expert", None, "tensor")
    rows = P(("dp", "expert"))
    both = P(("dp", "expert"), "tensor")
    expert_grads = P("expert", "dp", "tensor")
    return jax.shard_map(
        on_device,
        mesh=mesh,
        in_specs=(tokens, tokens, tokens, P())
        + (columns,) * 4
        + (P(), P())
        + (experts,) * 3
        + (tokens,),
        out_specs=(tokens, tokens, rows)
        + (both,) * 4
        + (rows, tokens)
        + (expert_grads,) * 3,
        check_vma=False,
    )
```

```python
import functools
import math

import jax
import jax.numpy as jnp
import numpy as np
from jax import lax
from jax.experimental import pallas as pl
from jax.experimental.pallas import tpu as pltpu
from jax.sharding import PartitionSpec as P

HD = 64
EPSILON = 1e-06
F32 = jnp.float32
BF16 = jnp.bfloat16
EXTRA = 128


def dot(left, right, dims):
    return lax.dot_general(left, right, (dims, ((), ())), preferred_element_type=F32)


def rope_tables(rows):
    inverse = np.exp(np.arange(HD // 2).astype(np.float32) * np.float32(-2.0 * math.log(1e4) / HD))
    angles = np.arange(rows, dtype=np.float32)[:, None] * inverse.astype(np.float32)[None, :]
    cosine, sine = np.cos(angles), np.sin(angles)
    return (
        jnp.asarray(np.concatenate([cosine] * 4, 1), F32),
        jnp.asarray(np.concatenate([-sine, sine] * 2, 1), F32),
    )


def other_halves(values):
    width = values.shape[1]
    lane = lax.broadcasted_iota(jnp.int32, values.shape, 1)
    return jnp.where(
        lane % HD < HD // 2,
        pltpu.roll(values, width - HD // 2, 1),
        pltpu.roll(values, HD // 2, 1),
    )


def widened(table, width):
    copies = width // table.shape[1]
    return table if copies == 1 else jnp.concatenate([table] * copies, 1)


def rotate(values, cosine, sine):
    width = values.shape[1]
    return values * widened(cosine, width) + other_halves(values) * widened(sine, width)


def rotate_back(values, cosine, sine):
    width = values.shape[1]
    return values * widened(cosine, width) - other_halves(values) * widened(sine, width)


def swap(x, axis, k):
    n = lax.axis_size(axis)
    return lax.ppermute(x, axis, [(i, i ^ k) for i in range(n)])


def swap_plane(x, k_dp, k_expert):
    n = lax.axis_size("expert")
    total = n * lax.axis_size("dp")
    return lax.ppermute(x, ("dp", "expert"), [(i, i ^ (k_dp * n + k_expert)) for i in range(total)])


def bits_of(n):
    k, out = n // 2, []
    while k >= 1:
        out.append(k)
        k //= 2
    return out


def gather_sets(x, near=None):
    bits = bits_of(lax.axis_size("expert"))
    sets = []
    for k_dp in range(lax.axis_size("dp")):
        if len(bits) == 2 and k_dp:
            parts = [swap(x, "dp", k_dp), swap_plane(x, k_dp, bits[0])]
            sets.append(parts + [swap(p, "expert", bits[1]) for p in parts])
            continue
        rows = swap(x, "dp", k_dp) if k_dp else x if near is None else near
        for k in bits[:-2]:
            rows = jnp.concatenate([rows, swap(rows, "expert", k)], 0)
        parts = [rows]
        for k in bits[-2:]:
            parts = parts + [swap(p, "expert", k) for p in parts]
        sets.append(parts)
    return sets


def swap_tensor(blocks):
    n = lax.axis_size("tensor")
    return [swap(blocks[k - 1], "tensor", k) for k in range(1, n)]


def gather_tensor(x):
    return [x] + swap_tensor([x] * (lax.axis_size("tensor") - 1))


def rows_at(index, rows):
    return pl.ds(pl.multiple_of(index * rows, rows), rows)


def plain_call(kernel, name, out_shape, scratch, flops, *arrays, after=(), hbm=(), vmem=16):
    def whole(a, far=False):
        if far:
            return pl.BlockSpec(memory_space=pltpu.HBM)
        if a.dtype == jnp.int32 and a.size <= 64:
            return pl.BlockSpec(memory_space=pltpu.SMEM)
        return pl.BlockSpec(a.shape, lambda i: (0,) * a.ndim)

    size = sum(a.size * a.dtype.itemsize for a in list(arrays) + list(out_shape))
    count, extra = len(arrays), len(after)

    def body(*refs):
        kernel(*refs[:count], *refs[count + extra :])

    arrays = list(arrays) + list(after)
    return pl.pallas_call(
        body,
        grid=(1,),
        in_specs=[whole(a, i in hbm) for i, a in enumerate(arrays[:count])] + [pl.BlockSpec(memory_space=pl.ANY)] * extra,
        out_specs=[whole(a) for a in out_shape],
        out_shape=out_shape,
        scratch_shapes=scratch,
        compiler_params=pltpu.CompilerParams(vmem_limit_bytes=vmem * 2**20),
        cost_estimate=pl.CostEstimate(flops=flops, bytes_accessed=size, transcendentals=0),
        name=name,
    )(*arrays)


def array(shape, dtype):
    return jax.ShapeDtypeStruct(shape, dtype)


def spread_blocks(me, value_ref, own_ref, sent_refs):
    rows = own_ref.shape[0]
    own_ref[...] = value_ref[rows_at(me, rows), :]
    for k, ref in enumerate(sent_refs, 1):
        ref[...] = value_ref[rows_at(me ^ k, rows), :].astype(ref.dtype)


def block_shapes(block, width, n):
    return [array((block, width), F32)] + [array((block, width), BF16)] * (n - 1)


def unit_rows(values):
    return lax.rsqrt(jnp.mean(values * values, -1, keepdims=True) + EPSILON)


def gain_row(ref):
    values = ref[...].astype(F32)
    return jnp.concatenate([values[i : i + 1, :] for i in range(values.shape[0])], 1)


def attend_kernel(heads, group, *refs):
    (meta, lengths, gain, cosine, sine) = refs[:5]
    far_refs, refs = refs[5:10], refs[10:]
    n1_ref, qkv_ref, prob_ref, att_ref, cos_ref, sin_ref = refs[:6]
    own_ref, *sent_refs = refs[6:-7]
    part_scr, hidden, query_w, key_w, value_w, output_w, sems = refs[-7:]
    near_refs = [hidden, query_w, key_w, value_w, output_w]
    copies = [
        pltpu.make_async_copy(far, near, sems.at[i])
        for i, (far, near) in enumerate(zip(far_refs, near_refs))
    ]
    for copy in copies:
        copy.start()
    copies[0].wait()
    x = hidden[...].astype(F32)
    n1 = (x * unit_rows(x) * gain_row(gain)).astype(BF16)
    n1_ref[...] = n1
    tokens = x.shape[0]
    rows = lax.broadcasted_iota(jnp.int32, (tokens, tokens), 0)
    columns = lax.broadcasted_iota(jnp.int32, (tokens, tokens), 1)
    table_rows = lax.broadcasted_iota(jnp.int32, cosine.shape, 0)
    cos, sin = cosine[...], sine[...]
    row_segment, column_segment = jnp.zeros_like(rows), jnp.zeros_like(rows)
    end = 0
    for i in range(lengths.shape[1] - 1):
        end = end + lengths[0, i]
        row_segment += (rows >= end).astype(jnp.int32)
        column_segment += (columns >= end).astype(jnp.int32)
        cos = jnp.where(table_rows >= end, pltpu.roll(cosine[...], end, 0), cos)
        sin = jnp.where(table_rows >= end, pltpu.roll(sine[...], end, 0), sin)
    cos_ref[...] = cos
    sin_ref[...] = sin
    allowed = (row_segment == column_segment) & (columns <= rows)
    q_width, kv_width = query_w.shape[1], key_w.shape[1]
    keys_at, values_at = q_width, q_width + kv_width
    for copy in copies[1:4]:
        copy.wait()
    qkv_ref[:, :q_width] = rotate(dot(n1, query_w[...], ((1,), (0,))), cos, sin).astype(BF16)
    qkv_ref[:, keys_at:values_at] = rotate(dot(n1, key_w[...], ((1,), (0,))), cos, sin).astype(BF16)
    qkv_ref[:, values_at:] = dot(n1, value_w[...], ((1,), (0,))).astype(BF16)
    for h in range(heads):
        g = h // group
        scores = dot(
            qkv_ref[:, h * HD : (h + 1) * HD],
            qkv_ref[:, keys_at + g * HD : keys_at + (g + 1) * HD],
            ((1,), (1,)),
        )
        masked = jnp.where(allowed, scores * HD ** (-0.5), -1e30)
        exponent = jnp.exp(masked - jnp.max(masked, -1, keepdims=True))
        prob = exponent / jnp.sum(exponent, -1, keepdims=True)
        prob_ref[h] = prob
        head_out = dot(
            prob.astype(BF16), qkv_ref[:, values_at + g * HD : values_at + (g + 1) * HD], ((1,), (0,))
        )
        att_ref[:, h * HD : (h + 1) * HD] = head_out.astype(BF16)
    for copy in copies[4:]:
        copy.wait()
    part_scr[...] = dot(att_ref[...], output_w[...], ((1,), (1,)))
    spread_blocks(meta[0], part_scr, own_ref, sent_refs)
    own_ref[...] += hidden[rows_at(meta[0], own_ref.shape[0]), :].astype(F32)


def fill_routes(routes, out_ref):
    width = out_ref.shape[1] - EXTRA
    named = routes[...].astype(F32).T
    lane = lax.broadcasted_iota(jnp.int32, (out_ref.shape[0], EXTRA), 1).astype(F32)
    total = jnp.zeros(lane.shape, F32)
    for j in range(named.shape[1]):
        total += (named[:, j : j + 1] == lane).astype(F32)
    out_ref[:, width:] = total.astype(BF16)


def second_norm_kernel(gain, grad, *refs):
    parts, (residual_ref, n2_ref, grad_ref) = refs[:-3], refs[-3:]
    grad_ref[...] = grad[...]
    residual = parts[0][...]
    for part in parts[1:]:
        residual = residual + part[...].astype(F32)
    residual_ref[...] = residual
    n2_ref[...] = (residual * unit_rows(residual) * gain_row(gain)).astype(BF16)


def place_second_kernel(meta, routes, *refs):
    blocks, out_ref = refs[:-1], refs[-1]
    rows, width = blocks[0].shape
    for k, ref in enumerate(blocks):
        out_ref[rows_at(meta[0] ^ k, rows), :width] = ref[...]
    fill_routes(routes, out_ref)


def halves_kernel(meta, near, got, last, *refs):
    own_ref, *sent_refs = refs[:-1]
    total_scr = refs[-1]
    rows = last.shape[0]
    total_scr[...] = (
        near[:rows, :].astype(F32) + got[:rows, :].astype(F32) + last[...].astype(F32)
    )
    spread_blocks(meta[0], total_scr, own_ref, sent_refs)


def residual_grad_kernel(experts, tensor_n, meta, residual_ref, n2_ref, dy_ref, router, gain, *refs):
    mixed_near, mixed_got, mixed_last = refs[:3]
    parts, refs = refs[3 : 3 + tensor_n], refs[3 + tensor_n :]
    dh_ref, gain_row_ref, message_ref, mixed_ref, *sent_refs = refs[:-1]
    mixed_scr = refs[-1]
    tokens = dy_ref.shape[0]
    mixed_scr[...] = (
        mixed_near[:tokens, :].astype(F32)
        + mixed_got[:tokens, :].astype(F32)
        + mixed_last[...].astype(F32)
    )
    block, width = residual_ref.shape
    mine = rows_at(meta[0], block)
    arrival = parts[0][...]
    for part in parts[1:]:
        arrival = arrival + part[...].astype(F32)
    logits = dot(n2_ref[mine, :width], router[...], ((1,), (1,)))
    routed = n2_ref[mine, width : width + experts].astype(F32) > 0.5
    logits = jnp.where(routed, logits, -1e30)
    gates = jnp.exp(logits - jnp.max(logits, -1, keepdims=True))
    gates = gates / jnp.sum(gates, -1, keepdims=True)
    extra = arrival[:, width:]
    dg = extra[:, :experts] + pltpu.roll(extra, EXTRA - experts, 1)[:, :experts]
    dlog = gates * (dg - jnp.sum(gates * dg, -1, keepdims=True))
    high = dlog.astype(BF16)
    low = (dlog - high.astype(F32)).astype(BF16)
    dn2 = (
        arrival[:, :width]
        + dot(high, router[...], ((1,), (0,)))
        + dot(low, router[...], ((1,), (0,)))
    )
    residual = residual_ref[...]
    scale = unit_rows(residual)
    hat = residual * scale
    gain_row_ref[...] = jnp.zeros_like(gain_row_ref)
    gain_row_ref[0:1, :] = jnp.sum(dn2 * hat, 0, keepdims=True)
    gained = dn2 * gain_row(gain)
    dh = dy_ref[mine, :].astype(F32) + scale * (
        gained - hat * jnp.mean(gained * hat, -1, keepdims=True)
    )
    dh_ref[...] = dh
    message_ref[:, :width] = dh.astype(BF16)
    message_ref[:, width:] = jnp.zeros((block, EXTRA), BF16)
    message_ref[:, width : width + experts] = high
    message_ref[:, width + experts : width + 2 * experts] = low
    mixed_ref[...] = mixed_scr[mine, :]
    for k, ref in enumerate(sent_refs, 1):
        ref[:, : width + EXTRA] = message_ref[...]
        ref[:, width + EXTRA :] = mixed_scr[rows_at(meta[0] ^ k, block), :].astype(BF16)


def attend_grad_kernel(heads, group, experts, expert_n, dp_n, tensor_n, *refs):
    (meta, hidden, gain_row, n1_ref, n2_ref, qkv_ref, prob_ref, att_ref, cos_ref, sin_ref) = refs[:10]
    query_w, key_w, value_w, output_w = refs[10:14]
    messages = refs[14 : 14 + tensor_n]
    mixed_own, residual_ref = refs[14 + tensor_n : 16 + tensor_n]
    near_ref, far_ref, layer_ref, own_ref, *sent_refs = refs[16 + tensor_n : -6]
    dh_scr, dqkv_scr, raw_scr, dn1_scr, left_scr, side_scr = refs[-6:]
    block = messages[0].shape[0]
    width = hidden.shape[1]
    for k, ref in enumerate(messages):
        dh_scr[rows_at(meta[0] ^ k, block), :] = ref[:, : width + EXTRA]
    cos, sin = cos_ref[...], sin_ref[...]
    q_width, kv_width = query_w.shape[1], key_w.shape[1]
    keys_at, values_at = q_width, q_width + kv_width
    dob = dh_scr[:, :width]
    da = dot(dob, output_w[...], ((1,), (0,))).astype(BF16)
    scale = HD ** (-0.5)
    for g in range(heads // group):
        key = qkv_ref[:, keys_at + g * HD : keys_at + (g + 1) * HD]
        value = qkv_ref[:, values_at + g * HD : values_at + (g + 1) * HD]
        dk = dv = 0.0
        for h in range(g * group, (g + 1) * group):
            da_h = da[:, h * HD : (h + 1) * HD]
            prob = prob_ref[h]
            dprob = dot(da_h, value, ((1,), (1,)))
            ds = prob * (dprob - jnp.sum(prob * dprob, -1, keepdims=True))
            raw_scr[:, h * HD : (h + 1) * HD] = dot(ds.astype(BF16), key, ((1,), (0,))) * scale
            dk = dk + dot(ds.T.astype(BF16), qkv_ref[:, h * HD : (h + 1) * HD], ((1,), (0,)))
            dv = dv + dot(prob.T.astype(BF16), da_h, ((1,), (0,)))
        raw_scr[:, keys_at + g * HD : keys_at + (g + 1) * HD] = dk * scale
        dqkv_scr[:, values_at + g * HD : values_at + (g + 1) * HD] = dv.astype(BF16)
    dqkv_scr[:, :q_width] = rotate_back(raw_scr[:, :q_width], cos, sin).astype(BF16)
    dqkv_scr[:, keys_at:values_at] = rotate_back(raw_scr[:, keys_at:values_at], cos, sin).astype(BF16)
    dn1 = (
        dot(dqkv_scr[:, :q_width], query_w[...], ((1,), (1,)))
        + dot(dqkv_scr[:, keys_at:values_at], key_w[...], ((1,), (1,)))
        + dot(dqkv_scr[:, values_at:], value_w[...], ((1,), (1,)))
    )
    dn1_scr[...] = dn1
    layer = residual_ref[...] + mixed_own[...]
    for ref in messages[1:]:
        layer = layer + ref[:, width + EXTRA :].astype(F32)
    layer_ref[...] = layer.astype(BF16)
    own_ref[...] = dn1_scr[rows_at(meta[0], block), :]
    for k, ref in enumerate(sent_refs, 1):
        ref[:, :width] = dn1_scr[rows_at(meta[0] ^ k, block), :].astype(BF16)
        ref[:, width:] = layer.astype(BF16)
    x = hidden[...].astype(F32)
    first_row = jnp.sum(dn1 * (x * unit_rows(x)), 0, keepdims=True)
    dlog_t = dh_scr[:, width:].astype(F32).T.astype(BF16)
    router_t = dot(dlog_t, n2_ref[:, :width], ((1,), (0,)))
    router_t = router_t[:experts] + router_t[experts : 2 * experts]
    side = jnp.concatenate(
        [router_t, gain_row[0:1, :], first_row, jnp.zeros((EXTRA - experts - 2, width), F32)], 0
    )
    side_scr[...] = side.T.astype(BF16)
    left_scr[:width, :] = n1_ref[...].T
    left_scr[width:, :] = dob.T
    places = expert_n * dp_n
    rows = width // places
    expert_bits = list(reversed(bits_of(expert_n)))
    qkv_width = values_at + kv_width
    for at in range(places):
        bits = [(at // (places >> (i + 1))) % 2 for i in range(len(expert_bits))]
        e_rel = sum(b * k for b, k in zip(bits, expert_bits))
        index = (meta[2] ^ (at % dp_n)) * expert_n + (meta[1] ^ e_rel)
        out = near_ref if at < places // 2 else far_ref
        to = slice((at % (places // 2)) * rows, (at % (places // 2) + 1) * rows)
        source = rows_at(index, rows)
        out[to, :qkv_width] = dot(left_scr[source, :], dqkv_scr[...], ((1,), (0,))).astype(BF16)
        out[to, qkv_width : qkv_width + EXTRA] = side_scr[source, :]
        below = left_scr[rows_at(index + places, rows), :]
        out[to, qkv_width + EXTRA :] = dot(below, att_ref[...], ((1,), (0,))).astype(BF16)


def input_grad_kernel(meta, hidden, gain, dh_ref, gains_ref, *refs):
    parts, out_ref = refs[:-1], refs[-1]
    block, width = dh_ref.shape
    dn1 = parts[0][...]
    for part in parts[1:]:
        dn1 = dn1 + part[:, :width].astype(F32)
    x = hidden[rows_at(meta[0], block), :].astype(F32)
    scale = unit_rows(x)
    hat = x * scale
    gained = dn1 * gain_row(gain)
    grad = dh_ref[...] + scale * (gained - hat * jnp.mean(gained * hat, -1, keepdims=True))
    out_ref[:, :width] = grad.astype(BF16)
    rows, columns = gains_ref.shape
    gains = gains_ref[...]
    high = gains.astype(BF16).astype(F32)
    out_ref[:, width:] = jnp.zeros((block, EXTRA), BF16)
    out_ref[: 2 * rows, width : width + columns] = jnp.concatenate(
        [high, gains - high], 0
    ).astype(BF16)


def place_last_kernel(tensor_n, meta, layer_own, *refs):
    layers, blocks = refs[: tensor_n - 1], refs[tensor_n - 1 : -4]
    layer_ref, grad_ref, first_ref, second_ref = refs[-4:]
    rows, width = layer_own.shape
    layer_ref[rows_at(meta[0], rows), :] = layer_own[...]
    for k, ref in enumerate(layers, 1):
        layer_ref[rows_at(meta[0] ^ k, rows), :] = ref[:, width:]
    gains = 0.0
    for k, ref in enumerate(blocks):
        grad_ref[rows_at(meta[0] ^ k, rows), :] = ref[:, :width].astype(F32)
        gains = gains + ref[:16, width:].astype(F32)
    gains = gains[:8] + gains[8:]
    columns = first_ref.shape[1]
    second_ref[...] = gains[0:1, :columns]
    first_ref[...] = gains[1:2, :columns]


def half_kernel(near, got, out_ref):
    half = out_ref.shape[0]
    out_ref[...] = (near[half:, :].astype(F32) + got[half:, :].astype(F32)).astype(BF16)


def add_kernel(near, got, own_ref, *sent_refs):
    rows = own_ref.shape[0]
    for k, ref in enumerate([own_ref] + list(sent_refs)):
        at = slice(k * rows, (k + 1) * rows)
        ref[...] = (near[at, :].astype(F32) + got[at, :].astype(F32)).astype(ref.dtype)


def last_kernel(experts, q_width, kv_width, *refs):
    parts, outs = refs[:-6], refs[-6:]
    total = parts[0][...]
    for part in parts[1:]:
        total = total + part[...].astype(F32)
    at = 0
    for ref, width in zip(outs[:3], (q_width, kv_width, kv_width)):
        ref[...] = total[:, at : at + width]
        at += width
    side = total[:, at : at + EXTRA]
    outs[3][...] = total[:, at + EXTRA :]
    side = side.T
    outs[4][...] = side[:experts]
    outs[5][...] = side[experts : experts + 8]


def pair_of(local_experts):
    return 2 if local_experts % 2 == 0 else 1


def kernel_params(tokens, vmem=28):
    return pltpu.CompilerParams(vmem_limit_bytes=(vmem if tokens <= 512 else 60) * 2**20)


def side_by_side(ref, first, count):
    parts = [ref[first + i] for i in range(count)]
    return parts[0] if count == 1 else jnp.concatenate(parts, 1)


def split_rows(chunk, chunks, value, near_ref, far_ref):
    if chunks == 1:
        half = value.shape[0] // 2
        near_ref[...] = value[:half]
        far_ref[...] = value[half:]
        return
    rows = value.shape[0]

    @pl.when(chunk < chunks // 2)
    def _():
        near_ref[pl.ds(pl.multiple_of(chunk * rows, rows), rows), :] = value

    @pl.when(chunk >= chunks // 2)
    def _():
        at = (chunk - chunks // 2) * rows
        far_ref[pl.ds(pl.multiple_of(at, rows), rows), :] = value


def expert_kernel(own, steps, pair, experts, parts, extra, *refs):
    meta_ref, refs = refs[0], refs[1:]
    x_parts, dy_parts, refs = refs[:parts], refs[parts : 2 * parts], refs[2 * parts :]
    gate_ref, up_ref, down_ref, router_ref = refs[:4]
    refs = refs[extra:]
    both_ref, gated_ref = refs[4:6]
    if own:
        dg_ref, dg_scr = refs[6], refs[-1]
        refs = refs[7:-1]
    else:
        refs = refs[6:]
    gates_scr, x_ref, dy_ref = refs
    step = pl.program_id(1)
    width = dy_ref.shape[1]
    lanes = gates_scr.shape[1]

    @pl.when(step == 0)
    def _():
        part_rows = x_parts[0].shape[0]
        for n in range(parts):
            x_ref[n * part_rows : (n + 1) * part_rows, :] = x_parts[n][...]
            dy_ref[n * part_rows : (n + 1) * part_rows, :] = dy_parts[n][...]
        logits = dot(x_ref[:, :width], router_ref[...], ((1,), (1,)))
        routed = x_ref[:, width : width + experts].astype(F32) > 0.5
        logits = jnp.where(routed, logits, -1e30)
        weights = jnp.exp(logits - jnp.max(logits, -1, keepdims=True))
        gates_scr[...] = jnp.zeros_like(gates_scr)
        gates_scr[:, :experts] = weights / jnp.sum(weights, -1, keepdims=True)
        if own:
            dg_scr[...] = jnp.zeros_like(dg_scr)

    first = meta_ref[1] * (pair * steps) + step * pair
    gates = pltpu.roll(gates_scr[...], lax.rem(lanes - first, lanes), 1)
    raw_all = dot(dy_ref[...], side_by_side(down_ref, 0, pair), ((1,), (0,)))
    units = gate_ref.shape[2]
    column = lax.broadcasted_iota(jnp.int32, gates.shape, 1)
    weight = jnp.concatenate([r[i] for i in range(pair) for r in (gate_ref, up_ref)], 1)
    both_all = dot(x_ref[:, :width], weight, ((1,), (0,)))
    for i in range(pair):
        gate_proj = both_all[:, 2 * i * units : (2 * i + 1) * units]
        up_proj = both_all[:, (2 * i + 1) * units : (2 * i + 2) * units]
        raw = raw_all[:, i * units : (i + 1) * units]
        mine = gates[:, i : i + 1]
        sigmoid_gate = 0.5 * jnp.tanh(0.5 * gate_proj) + 0.5
        activated = gate_proj * sigmoid_gate
        hidden = activated * up_proj
        grad_hidden = raw * mine
        grad_gate = grad_hidden * up_proj * (sigmoid_gate + activated * (1.0 - sigmoid_gate))
        at = 2 * i * units
        both_ref[:, at : at + units] = grad_gate.astype(BF16)
        both_ref[:, at + units : at + 2 * units] = (grad_hidden * activated).astype(BF16)
        gated_ref[:, i * units : (i + 1) * units] = (hidden * mine).astype(BF16)
        if own:
            dg = jnp.sum(raw * hidden, 1, keepdims=True)
            dg_scr[...] += jnp.where(column == first + i, dg, 0.0)
    if own:

        @pl.when(step == steps - 1)
        def _():
            dg = dg_scr[...]
            high = dg.astype(BF16).astype(F32)
            low = pltpu.roll(dg - high, experts, 1)
            dg_ref[...] = (high + low).astype(BF16)


def expert_call(own, meta, xs, dys, gate_weight, up_weight, down_weight, router_weight, after=()):
    part_rows, width = dys[0].shape
    parts = len(xs)
    tokens = part_rows * parts
    if tokens > 512:
        xs, dys, parts = [jnp.concatenate(xs, 0)], [jnp.concatenate(dys, 0)], 1
        part_rows = tokens
    x_width = xs[0].shape[1]
    local, _, units = gate_weight.shape
    experts = router_weight.shape[0]
    pair = pair_of(local)
    rows = min(tokens, 512)
    chunks, steps = tokens // rows, local // pair
    grid_spec = dict(
        grid=(chunks, steps),
        in_specs=[
            pl.BlockSpec(memory_space=pltpu.SMEM),
        ]
        + [pl.BlockSpec((rows // parts, x_width), lambda c, s: (c, 0))] * parts
        + [pl.BlockSpec((rows // parts, width), lambda c, s: (c, 0))] * parts
        + [pl.BlockSpec((pair, width, units), lambda c, s: (s, 0, 0))] * 3
        + [pl.BlockSpec(router_weight.shape, lambda c, s: (0, 0))]
        + [pl.BlockSpec(memory_space=pl.ANY)] * len(after),
        out_specs=[
            pl.BlockSpec((rows, pair * 2 * units), lambda c, s: (c, s)),
            pl.BlockSpec((rows, pair * units), lambda c, s: (c, s)),
        ],
        scratch_shapes=[
            pltpu.VMEM((rows, 128), F32),
            pltpu.VMEM((rows, x_width), BF16),
            pltpu.VMEM((rows, width), BF16),
        ],
    )
    out_shape = [
        jax.ShapeDtypeStruct((tokens, local * 2 * units), BF16),
        jax.ShapeDtypeStruct((tokens, local * units), BF16),
    ]
    if own:
        grid_spec["out_specs"] += [pl.BlockSpec((rows, EXTRA), lambda c, s: (c, 0))]
        out_shape += [jax.ShapeDtypeStruct((tokens, EXTRA), BF16)]
        grid_spec["scratch_shapes"] += [pltpu.VMEM((rows, 128), F32)]
    products = 3
    return pl.pallas_call(
        functools.partial(expert_kernel, own, steps, pair, experts, parts, len(after)),
        out_shape=out_shape,
        compiler_params=kernel_params(tokens),
        cost_estimate=pl.CostEstimate(
            flops=2 * products * tokens * width * local * units,
            bytes_accessed=2 * (3 * local * width * units + 3 * tokens * width),
            transcendentals=tokens * local * units,
        ),
        name="experts_own" if own else "experts_far",
        **grid_spec,
    )(meta, *xs, *dys, gate_weight, up_weight, down_weight, router_weight, *after)


def arrival_kernel(chunks, steps, pair, both_ref, dg_ref, gate_ref, up_ref, *refs):
    near_ref, far_ref, total_scr = refs[-3:]
    chunk, step = pl.program_id(0), pl.program_id(1)

    @pl.when(step == 0)
    def _():
        total_scr[...] = jnp.zeros_like(total_scr)

    weight = jnp.concatenate([r[i] for i in range(pair) for r in (gate_ref, up_ref)], 1)
    total_scr[...] += dot(both_ref[...], weight, ((1,), (1,)))

    @pl.when(step == steps - 1)
    def _():
        message = jnp.concatenate([total_scr[...].astype(BF16), dg_ref[...]], 1)
        split_rows(chunk, chunks, message, near_ref, far_ref)


def arrival_call(both, dg, gate_weight, up_weight, after=()):
    tokens = both.shape[0]
    local, width, units = gate_weight.shape
    pair = pair_of(local)
    rows = min(tokens, 512)
    chunks, steps = tokens // rows, local // pair
    half = (tokens // 2, width + EXTRA)
    return pl.pallas_call(
        functools.partial(arrival_kernel, chunks, steps, pair),
        grid=(chunks, steps),
        in_specs=[
            pl.BlockSpec((rows, pair * 2 * units), lambda c, s: (c, s)),
            pl.BlockSpec((rows, EXTRA), lambda c, s: (c, 0)),
        ]
        + [pl.BlockSpec((pair, width, units), lambda c, s: (s, 0, 0))] * 2
        + [pl.BlockSpec(memory_space=pl.ANY)] * len(after),
        out_specs=[pl.BlockSpec(half, lambda c, s: (0, 0))] * 2,
        out_shape=[jax.ShapeDtypeStruct(half, BF16)] * 2,
        scratch_shapes=[pltpu.VMEM((rows, width), F32)],
        compiler_params=kernel_params(tokens),
        cost_estimate=pl.CostEstimate(
            flops=4 * tokens * width * local * units,
            bytes_accessed=4 * (local * width * units + 2 * tokens * width),
            transcendentals=0,
        ),
        name="experts_arrival",
    )(both, dg, gate_weight, up_weight, *after)


def mixed_kernel(chunks, steps, pair, gated_ref, down_ref, *refs):
    near_ref, far_ref, total_scr = refs[-3:]
    chunk, step = pl.program_id(0), pl.program_id(1)

    @pl.when(step == 0)
    def _():
        total_scr[...] = jnp.zeros_like(total_scr)

    total_scr[...] += dot(gated_ref[...], side_by_side(down_ref, 0, pair), ((1,), (1,)))

    @pl.when(step == steps - 1)
    def _():
        split_rows(chunk, chunks, total_scr[...].astype(BF16), near_ref, far_ref)


def mixed_call(gated, down_weight, after=()):
    tokens = gated.shape[0]
    local, width, units = down_weight.shape
    pair = pair_of(local)
    rows = min(tokens, 512)
    chunks, steps = tokens // rows, local // pair
    half = (tokens // 2, width)
    return pl.pallas_call(
        functools.partial(mixed_kernel, chunks, steps, pair),
        grid=(chunks, steps),
        in_specs=[
            pl.BlockSpec((rows, pair * units), lambda c, s: (c, s)),
            pl.BlockSpec((pair, width, units), lambda c, s: (s, 0, 0)),
        ]
        + [pl.BlockSpec(memory_space=pl.ANY)] * len(after),
        out_specs=[pl.BlockSpec(half, lambda c, s: (0, 0))] * 2,
        out_shape=[jax.ShapeDtypeStruct(half, BF16)] * 2,
        scratch_shapes=[pltpu.VMEM((rows, width), F32)],
        compiler_params=kernel_params(tokens),
        cost_estimate=pl.CostEstimate(
            flops=2 * tokens * width * local * units,
            bytes_accessed=2 * (local * width * units + 2 * tokens * width),
            transcendentals=0,
        ),
        name="experts_mixed",
    )(gated, down_weight, *after)


def weight_grad_kernel(sets, parts, outs, pair, units, place_ref, *refs):
    lefts, rights = refs[: sets * parts], refs[sets * parts : sets * parts + sets]
    grad_refs, token_ref = refs[-4 - outs : -4], refs[-4]
    left_scr, out_scr, sems = refs[-3:]
    token_ref[...] = jnp.zeros_like(token_ref)
    step, steps = pl.program_id(0), pl.num_programs(0)
    slot = lax.rem(step, 2)

    def copies(at, which):
        return [
            pltpu.make_async_copy(
                out_scr.at[which, j], grad_refs[j].at[pl.ds(at * pair, pair)], sems.at[which, j]
            )
            for j in range(outs)
        ]

    @pl.when(pl.program_id(0) == 0)
    def _():
        for n in range(sets * parts):
            rows = lefts[n].shape[0]
            left_scr[:, n * rows : (n + 1) * rows] = lefts[n][...].T

    rows = rights[0].shape[0]
    total = None
    for n in range(sets):
        part = dot(left_scr[:, n * rows : (n + 1) * rows], rights[n][...], ((1,), (0,)))
        total = part if total is None else total + part

    @pl.when(step >= 2)
    def _():
        for copy in copies(step - 2, slot):
            copy.wait()

    for i in range(pair):
        for j in range(outs):
            at = (i * outs + j) * units
            out_scr[slot, j, i] = total[:, at : at + units]
    for copy in copies(step, slot):
        copy.start()

    @pl.when(step == steps - 1)
    def _():
        for copy in copies(step, slot):
            copy.wait()

    @pl.when((step == steps - 1) & (step >= 1))
    def _():
        for copy in copies(step - 1, 1 - slot):
            copy.wait()


def weight_grad_call(meta, lefts, rights, local, units, after=()):
    sets, parts = len(lefts), len(lefts[0])
    outs = rights[0].shape[1] // (local * units)
    part_rows = lefts[0][0].shape[0]
    width = lefts[0][0].shape[1] // 128 // sets * 128
    tokens = part_rows * parts
    lefts = sum(lefts, [])
    pair = pair_of(local)
    columns = pl.BlockSpec(
        (part_rows, width), lambda s, meta: (0, meta[2]), pipeline_mode=pl.Buffered(1)
    )
    return pl.pallas_call(
        functools.partial(weight_grad_kernel, sets, parts, outs, pair, units),
        grid_spec=pltpu.PrefetchScalarGridSpec(
            num_scalar_prefetch=1,
            grid=(local // pair,),
            in_specs=[columns] * (sets * parts)
            + [pl.BlockSpec((tokens, pair * outs * units), lambda s, meta: (0, s))] * sets
            + [pl.BlockSpec(memory_space=pl.ANY)] * len(after),
            out_specs=[pl.BlockSpec(memory_space=pltpu.HBM)] * outs
            + [pl.BlockSpec((8, 128), lambda s, meta: (0, 0))],
            scratch_shapes=[
                pltpu.VMEM((width, sets * tokens), BF16),
                pltpu.VMEM((2, outs, pair, width, units), F32),
                pltpu.SemaphoreType.DMA((2, outs)),
            ],
        ),
        out_shape=[array((local, width, units), F32)] * outs + [array((8, 128), F32)],
        compiler_params=kernel_params(tokens),
        cost_estimate=pl.CostEstimate(
            flops=2 * sets * tokens * width * outs * local * units,
            bytes_accessed=4 * outs * local * width * units + 4 * sets * tokens * width,
            transcendentals=0,
        ),
        name="experts_weight_grads",
    )(meta, *lefts, *rights, *after)


def reduce_first(near, far, after=()):
    bits = list(reversed(bits_of(lax.axis_size("expert"))))
    for k in bits[:-2]:
        got = swap(far, "expert", k)
        total = (near.astype(F32) + got.astype(F32)).astype(BF16)
        near, far = jnp.split(total, 2, 0)
    got = swap(far, "expert", bits[-2])
    half = near.shape[0] // 2
    if after:
        (sent,) = plain_call(
            half_kernel,
            "half",
            [array((half, near.shape[1]), BF16)],
            [],
            near.size,
            near,
            got,
            after=after,
        )
    else:
        sent = (near[half:].astype(F32) + got[half:].astype(F32)).astype(BF16)
    return near, got, swap(sent, "expert", bits[-1])


def on_device(
    hidden_in,
    seq_lengths,
    expert_routes,
    first_gain,
    query_weight,
    key_weight,
    value_weight,
    output_weight,
    second_gain,
    router_weight,
    gate_weight,
    up_weight,
    down_weight,
    grad_layer_out,
):
    tokens_here, model_width = hidden_in.shape
    q_width, kv_width = query_weight.shape[1], key_weight.shape[1]
    heads, group = q_width // HD, q_width // kv_width
    expert_count = router_weight.shape[1]
    local_experts, _, units = gate_weight.shape
    tensor_n = lax.axis_size("tensor")
    expert_n = lax.axis_size("expert")
    dp_n = lax.axis_size("dp")
    block = tokens_here // tensor_n
    meta = jnp.stack([lax.axis_index(a) for a in ("tensor", "expert", "dp")]).astype(jnp.int32)
    first_tile, second_tile = first_gain.reshape(-1, 128), second_gain.reshape(-1, 128)

    cosine, sine = rope_tables(tokens_here)
    blocks = block_shapes(block, model_width, tensor_n)
    outs = plain_call(
        functools.partial(attend_kernel, heads, group),
        "attend",
        [
            array((tokens_here, model_width), BF16),
            array((tokens_here, q_width + 2 * kv_width), BF16),
            array((heads, tokens_here, tokens_here), F32),
            array((tokens_here, q_width), BF16),
            array(cosine.shape, F32),
            array(sine.shape, F32),
        ]
        + blocks,
        [
            pltpu.VMEM((tokens_here, model_width), F32),
            pltpu.VMEM(hidden_in.shape, BF16),
            pltpu.VMEM(query_weight.shape, BF16),
            pltpu.VMEM(key_weight.shape, BF16),
            pltpu.VMEM(value_weight.shape, BF16),
            pltpu.VMEM(output_weight.shape, BF16),
            pltpu.SemaphoreType.DMA((5,)),
        ],
        2 * tokens_here * model_width * 3 * q_width,
        meta,
        seq_lengths,
        first_tile,
        cosine,
        sine,
        hidden_in,
        query_weight,
        key_weight,
        value_weight,
        output_weight,
        hbm=range(5, 10),
        vmem=60,
    )
    n1, qkv, prob, att, cosine, sine, part, *sent = outs
    far_grads = [swap(grad_layer_out, "dp", k) for k in range(1, dp_n)]
    if expert_n == 4:
        far_grads += [swap_plane(grad_layer_out, k, 2) for k in range(1, dp_n)]
    residual, second_block, grad_near = plain_call(
        second_norm_kernel,
        "second_norm",
        [
            array((block, model_width), F32),
            array((block, model_width), BF16),
            array(grad_layer_out.shape, BF16),
        ],
        [],
        8 * block * model_width,
        second_tile,
        grad_layer_out,
        part,
        *swap_tensor(sent),
        after=far_grads,
    )
    grad_sets = gather_sets(grad_layer_out, grad_near)
    (second_group,) = plain_call(
        place_second_kernel,
        "place_second",
        [array((tokens_here, model_width + EXTRA), BF16)],
        [],
        tokens_here * model_width,
        meta,
        expert_routes.T,
        *gather_tensor(second_block),
        after=grad_sets[0][1:2],
    )
    second_sets = gather_sets(second_group)

    router_t = router_weight.T
    weights = (gate_weight, up_weight, down_weight, router_t)
    far_grads = [g for x in grad_sets[1:] for g in x[:2]]
    own = expert_call(True, meta, second_sets[0], grad_sets[0], *weights, after=far_grads)
    arrival = arrival_call(
        own[0], own[2], gate_weight, up_weight, after=[x for y in second_sets[1:] for x in y[:2]]
    )
    sides = [own] + [
        expert_call(False, meta, second_sets[i], grad_sets[i], *weights) for i in range(1, dp_n)
    ]
    mixed = mixed_call(own[1], down_weight, after=arrival[:1])
    arrival = plain_call(
        halves_kernel,
        "arrival_blocks",
        block_shapes(block, model_width + EXTRA, tensor_n),
        [pltpu.VMEM((tokens_here, model_width + EXTRA), F32)],
        2 * tokens_here * model_width,
        meta,
        *reduce_first(*arrival),
        after=[mixed[0]] + [x[1] for x in sides[1:]],
    )
    mixed = reduce_first(*mixed, after=arrival[:1])
    arrival = [arrival[0]] + swap_tensor(arrival[1:])
    grad_down, down_done = weight_grad_call(
        meta, grad_sets, [x[1] for x in sides], local_experts, units
    )
    grad_gate, grad_upproj, gate_done = weight_grad_call(
        meta, second_sets, [x[0] for x in sides], local_experts, units
    )

    grad_resid, gain_row, message, mixed_own, *sent = plain_call(
        functools.partial(residual_grad_kernel, expert_count, tensor_n),
        "residual_grad",
        [
            array((block, model_width), F32),
            array((8, model_width), F32),
            array((block, model_width + EXTRA), BF16),
            array((block, model_width), F32),
        ]
        + [array((block, 2 * model_width + EXTRA), BF16)] * (tensor_n - 1),
        [pltpu.VMEM((tokens_here, model_width), F32)],
        20 * block * model_width,
        meta,
        residual,
        second_group,
        grad_layer_out,
        router_t,
        second_tile,
        *mixed,
        *arrival,
        after=[down_done],
    )
    places = expert_n * dp_n
    rows = model_width // places
    last_width = 2 * q_width + 2 * kv_width + EXTRA
    near, far, layer_block, *dn1 = plain_call(
        functools.partial(
            attend_grad_kernel, heads, group, expert_count, expert_n, dp_n, tensor_n
        ),
        "attend_grad",
        [array((model_width // 2, last_width), BF16)] * 2
        + [array((block, model_width), BF16), array((block, model_width), F32)]
        + [array((block, 2 * model_width), BF16)] * (tensor_n - 1),
        [
            pltpu.VMEM((tokens_here, model_width + EXTRA), BF16),
            pltpu.VMEM((tokens_here, q_width + 2 * kv_width), BF16),
            pltpu.VMEM((tokens_here, q_width + kv_width), F32),
            pltpu.VMEM((tokens_here, model_width), F32),
            pltpu.VMEM((2 * model_width, tokens_here), BF16),
            pltpu.VMEM((model_width, EXTRA), BF16),
        ],
        2 * tokens_here * model_width * 6 * q_width,
        meta,
        hidden_in,
        gain_row,
        n1,
        second_group,
        qkv,
        prob,
        att,
        cosine,
        sine,
        query_weight,
        key_weight,
        value_weight,
        output_weight,
        message,
        *swap_tensor(sent),
        mixed_own,
        residual,
        after=[gate_done],
    )

    dn1 = [dn1[0]] + swap_tensor(dn1[1:])

    expert_bits = list(reversed(bits_of(expert_n)))
    for k in expert_bits[:-2]:
        total = near.astype(F32) + swap(far, "expert", k).astype(F32)
        near, far = jnp.split(total.astype(BF16), 2, 0)
    got = swap(far, "expert", expert_bits[-2])
    shapes = [array((rows, last_width), F32)] + [array((rows, last_width), BF16)] * (2 * dp_n - 1)
    own_rows, *sent = plain_call(
        add_kernel, "plane_add", shapes, [], model_width * last_width, near, got
    )
    ways = [(k % dp_n, (k // dp_n) * expert_bits[-1]) for k in range(1, 2 * dp_n)]
    got = [swap_plane(x, *way) for x, way in zip(sent, ways)]
    grad_query, grad_key, grad_value, grad_outproj, grad_router, gains = plain_call(
        functools.partial(last_kernel, expert_count, q_width, kv_width),
        "plane_last",
        [
            array((rows, q_width), F32),
            array((rows, kv_width), F32),
            array((rows, kv_width), F32),
            array((rows, q_width), F32),
            array((expert_count, rows), F32),
            array((8, rows), F32),
        ],
        [],
        4 * rows * last_width,
        own_rows,
        *got,
        after=dn1[1:],
    )
    (last_block,) = plain_call(
        input_grad_kernel,
        "input_grad",
        [array((block, model_width + EXTRA), BF16)],
        [],
        10 * block * model_width,
        meta,
        hidden_in,
        first_tile,
        grad_resid,
        gains,
        *dn1,
    )
    layer_out, grad_input, grad_first_out, grad_second_out = plain_call(
        functools.partial(place_last_kernel, tensor_n),
        "place_last",
        [
            array((tokens_here, model_width), BF16),
            array((tokens_here, model_width), F32),
            array((1, rows), F32),
            array((1, rows), F32),
        ],
        [],
        tokens_here * model_width,
        meta,
        layer_block,
        *dn1[1:],
        *gather_tensor(last_block),
    )
    return (
        layer_out,
        grad_input,
        grad_first_out[0],
        grad_query,
        grad_key,
        grad_value,
        grad_outproj,
        grad_second_out[0],
        grad_router.T,
        grad_gate,
        grad_upproj,
        grad_down,
    )


def solution(mesh):
    tokens = P(("dp", "expert"), None)
    columns = P(None, "tensor")
    experts = P("expert", None, "tensor")
    rows = P(("dp", "expert"))
    both = P(("dp", "expert"), "tensor")
    expert_grads = P("expert", "dp", "tensor")
    return jax.shard_map(
        on_device,
        mesh=mesh,
        in_specs=(tokens, tokens, tokens, P())
        + (columns,) * 4
        + (P(), P())
        + (experts,) * 3
        + (tokens,),
        out_specs=(tokens, tokens, rows)
        + (both,) * 4
        + (rows, tokens)
        + (expert_grads,) * 3,
        check_vma=False,
    )
```
